128 devices in a mesh: dp: 4 (over y_hi, core), vocab: 32 (over x, z, y_lo).
Axes of the slice: x: 4, y: 4 (y_hi: 2, y_lo: 2; y = y_hi * 2 + y_lo), z: 4, core: 2. Of those that a mesh axis runs over, the one named last changes fastest.
Arguments:
- hidden_states: bfloat16 [256, 8192], P(('dp', 'vocab')), may hold values from -8 to 8
- head_weight: bfloat16 [8192, 65536], P(None, ('dp', 'vocab')), may hold values from -2 to 2
- teacher_codes: bfloat16 [256, 65536], P(('dp', 'vocab')), may hold values from -448 to 448, as said below
- teacher_scales: bfloat16 [256, 512], P(('dp', 'vocab')), may hold values from 0.5 to 1.5
- targets: int32 [256], replicated, may hold values from 0 to 65535
Outputs:
- hidden_grad: float32 [256, 8192], P(('dp', 'vocab'))
- head_grad: bfloat16 [8192, 65536], P(None, ('dp', 'vocab'))
- token_loss: float32 [256], replicated
The draws below stay inside these ranges and needn't reach their ends.
Inputs may be any that keep to these rules, and one draw needn't show every extreme that they name: `teacher_codes`: codes lie within the range of an 8-bit float.
All inputs are finite; a program needn't handle non-finite values.
Results may differ from the reference program's by a relative error of at most 0.0041.
Values may be sent and summed in bfloat16 or wider, within the bound.
A program may use at most 128 MiB of HBM per device.

```python
import math
import jax
import jax.numpy as jnp
from jax import lax

D = 8192
BLOCK = 128
TOKENS = 256
VOCAB = 65536


def draw_hidden_states(key, part):
    key = jax.random.fold_in(key, 1)
    values = jnp.clip(jax.random.normal(key, (TOKENS, D), jnp.float32), -5.0, 5.0)
    return values.astype(jnp.bfloat16)


def draw_head_weight(key, part):
    key = jax.random.fold_in(key, 2)
    noise = jnp.clip(jax.random.normal(key, (D, VOCAB), jnp.float32), -5.0, 5.0) * (3.0 / D ** 0.5)
    values = noise
    return values.astype(jnp.bfloat16)


def draw_teacher_codes(key, part):
    key = jax.random.fold_in(key, 3)
    values = jnp.clip(3.0 * jax.random.normal(key, (TOKENS, VOCAB), jnp.float32), -15.0, 15.0)
    return values.astype(jnp.bfloat16)


def touch_ends(values, rng, smallest, top_value):
    longest = values.shape.index(max(values.shape))
    spots = []
    for shift in (0, 1):
        where = [jax.random.randint(jax.random.fold_in(rng, axis), (), 0, length) for axis, length in enumerate(values.shape)]
        where[longest] = (where[longest] + shift) % values.shape[longest]
        spots.append(tuple(where))
    return values.at[spots[0]].set(smallest).at[spots[1]].set(top_value)


def level_of(own_key, dims, cuts, least, high):
    def one(position, shards_of):
        heights = jax.random.uniform(jax.random.fold_in(jax.random.fold_in(own_key, 6), position), (shards_of,), jnp.float32, least / len(cuts), high / len(cuts))
        return jnp.repeat(jnp.exp(heights), dims[position] // shards_of).reshape((-1,) + (1,) * (len(dims) - position - 1))

    factor_of = one(*cuts[0])
    for cut in cuts[1:]:
        factor_of = factor_of * one(*cut)
    return factor_of


def setup_inputs(seed: int = 0) -> dict:
    key_list = jax.random.split(jax.random.key(seed), 6)
    return {
        "hidden_states": draw_hidden_states(jax.random.fold_in(key_list[5], 71), 0),
        "head_weight": draw_head_weight(jax.random.fold_in(key_list[5], 71), 0),
        "teacher_codes": draw_teacher_codes(jax.random.fold_in(key_list[5], 71), 0),
        "teacher_scales": jnp.clip(jnp.exp(math.log(1.5) - 1.0986123 * jax.random.uniform(key_list[3], (TOKENS, VOCAB // BLOCK), jnp.float32) ** level_of(key_list[3], (TOKENS, VOCAB // BLOCK), ((0, 128),), -0.2, 0.2)), 0.5, 1.5).astype(jnp.bfloat16),
        "targets": touch_ends(jax.random.randint(key_list[4], (TOKENS,), 0, VOCAB), jax.random.fold_in(key_list[4], 1), 0, VOCAB - 1).astype(jnp.int32),
    }


GRAD_SCALE = 32.0
CE_WEIGHT = 0.5


def reference(hidden_states, head_weight, teacher_codes, teacher_scales, targets):
    blocked = teacher_codes.astype(jnp.float32).reshape(TOKENS, VOCAB // BLOCK, BLOCK)
    teacher = (blocked * teacher_scales.astype(jnp.float32)[:, :, None]).reshape(TOKENS, VOCAB)
    logits = jnp.dot(hidden_states, head_weight, preferred_element_type=jnp.float32)
    peak_student = jnp.max(logits, axis=1)
    peak_teacher = jnp.max(teacher, axis=1)
    log_student = peak_student + jnp.log(jnp.sum(jnp.exp(logits - peak_student[:, None]), axis=1))
    log_teacher = peak_teacher + jnp.log(jnp.sum(jnp.exp(teacher - peak_teacher[:, None]), axis=1))
    student_prob = jnp.exp(logits - log_student[:, None])
    teacher_prob = jnp.exp(teacher - log_teacher[:, None])
    columns = lax.broadcasted_iota(jnp.int32, (1, VOCAB), 1)
    target_hit = (columns == targets[:, None].astype(jnp.int32)).astype(jnp.float32)
    target_logit = jnp.sum(target_hit * logits, axis=1)
    token_loss = jnp.sum(teacher_prob * (teacher - logits), axis=1) - log_teacher + log_student + CE_WEIGHT * (log_student - target_logit)
    grad_logits = (GRAD_SCALE * ((1.0 + CE_WEIGHT) * student_prob - teacher_prob - CE_WEIGHT * target_hit)).astype(jnp.bfloat16)
    hidden_grad = jnp.dot(grad_logits, head_weight.T, preferred_element_type=jnp.float32)
    head_grad = jnp.dot(hidden_states.T, grad_logits, preferred_element_type=jnp.float32).astype(jnp.bfloat16)
    return hidden_grad, head_grad, token_loss
```

```python
import functools

import jax
import jax.numpy as jnp
from jax import lax
from jax.experimental import pallas as pl
from jax.experimental.pallas import tpu as pltpu
from jax.sharding import PartitionSpec as P

GRAD_SCALE = 32.0
CE_WEIGHT = 0.5
F32, BF16 = jnp.float32, jnp.bfloat16
MESH = pl.DeviceIdType.MESH
AXES = ("dp", "vocab")

CHUNK = 1024
WIDE = CHUNK + 128
PARTS = (
    (0, 384, 384, "xyz"),
    (384, 384, 384, "yzx"),
    (768, 384, 256, "zxy"),
)


def kernel(
    h_in, w_in, codes_in, scales_in, tgt_in,
    hg_out, loss_out, grad_out, h_out,
    h_all, w_all, src8, pre8, t1, t2, t3, t4, logits, teacher,
    st_core, st_x, st_y, st_z,
    own, send_c, recv_c, summed,
    r3a, r3b, r3c, f2a, f2b, f2c, b2a, b2b, b2c, r2a, r2b, r2c,
    f1a, f1b, f1c, r1a, r1b, r1c, fin_s, fin_r,
    send_sems, recv_sems, local_sems,
):
    dp, vo = lax.axis_index("dp"), lax.axis_index("vocab")
    me = {"x": vo // 8, "z": (vo // 2) % 4, "y": (dp // 2) * 2 + vo % 2, "c": dp % 2}

    def device(**other):
        at = {**me, **other}
        return ((at["y"] // 2) * 2 + at["c"], (at["x"] * 4 + at["z"]) * 2 + at["y"] % 2)

    def step(axis, k):
        return lax.rem(me[axis] + k, 2 if axis == "c" else 4)

    count = {"remote": 0, "local": 0}
    unsent = []

    def push(src, dst, **other):
        n = count["remote"]
        count["remote"] += 1
        copy = pltpu.make_async_remote_copy(
            src_ref=src, dst_ref=dst, send_sem=send_sems.at[n], recv_sem=recv_sems.at[n],
            device_id=device(**other), device_id_type=MESH,
        )
        copy.start()
        unsent.append(copy)
        return copy

    def local(src, dst):
        n = count["local"]
        count["local"] += 1
        copy = pltpu.make_async_copy(src, dst, local_sems.at[n])
        copy.start()
        return copy

    heads = []
    for c in range(2):
        for z in range(4):
            g = c * 4 + z
            heads.append(local(h_in.at[:, pl.ds(g * CHUNK, CHUNK)], src8.at[c, z, :, pl.ds(0, CHUNK)]))
            heads.append(local(scales_in.at[:, pl.ds(z * 128, 128)], src8.at[c, z, :, pl.ds(CHUNK, 128)]))
    own_codes = local(codes_in.at[:, :, me["x"]], t1.at[me["x"]])
    w_copy = local(w_in, w_all)

    barrier = pltpu.get_barrier_semaphore()
    partners = [dict(x=step("x", k)) for k in (1, 2, 3)] + [dict(y=step("y", k)) for k in (1, 2, 3)]
    partners += [dict(z=step("z", k), c=step("c", e)) for k in range(4) for e in range(2) if (k, e) != (0, 0)]
    for other in partners:
        pl.semaphore_signal(barrier, inc=1, device_id=device(**other), device_id_type=MESH)
    for copy in heads:
        copy.wait()
    pl.semaphore_wait(barrier, len(partners))

    arriving = []
    for k in range(4):
        for e in range(2):
            if (k, e) != (0, 0):
                z, c = step("z", k), step("c", e)
                arriving.append(push(src8.at[c, z], pre8.at[me["c"], me["z"]], z=z, c=c))
    pre8[me["c"], me["z"]] = src8[me["c"], me["z"]]
    for copy in arriving:
        copy.wait_recv()
    h_all[me["c"], me["z"], me["x"], me["y"]] = jnp.concatenate(
        [pre8[c, z].astype(F32) for z in range(4) for c in range(2)], axis=0
    ).astype(BF16)

    def gathered(part, free, **fixed):
        at = {**me, **fixed}
        index = [slice(None) if a in free else at[a] for a in "zxy"]
        return h_all.at[(me["c"], *index, slice(None), pl.ds(part[0], part[1]))]

    def gather_phase(part, p):
        order = part[3]
        view = gathered(part, order[:p])
        axis = order[p]
        return [push(view, view, **{axis: step(axis, k)}) for k in (1, 3, 2)]

    wave = [gather_phase(part, 0) for part in PARTS]
    codes_wave = [push(codes_in.at[:, :, step("x", k)], t1.at[me["x"]], x=step("x", k)) for k in (1, 3, 2)]
    for p in (1, 2):
        for i, part in enumerate(PARTS):
            for copy in wave[i]:
                copy.wait_recv()
            wave[i] = gather_phase(part, p)
        for copy in codes_wave:
            copy.wait_recv()
        if p == 1:
            own_codes.wait()
            codes_wave = [
                push(t1.at[:, step("y", k) // 2, :, :, step("y", k) % 2], t2.at[me["y"]], y=step("y", k))
                for k in (1, 3, 2)
            ]
            t2[me["y"]] = t1[:, me["y"] // 2, :, :, me["y"] % 2]
        else:
            codes_wave = [push(t2.at[:, :, :, step("z", k)], t3.at[me["z"]], z=step("z", k)) for k in (1, 3, 2)]
            t3[me["z"]] = t2[:, :, :, me["z"]]

    other_core = step("c", 1)
    crossing = []

    def cross(part, coordinate):
        view = gathered(part, part[3][:2], **{part[3][2]: coordinate})
        crossing.append(push(view, view, c=other_core))

    for part in PARTS:
        cross(part, me[part[3][2]])
    for n, k in enumerate((1, 3, 2)):
        for i, part in enumerate(PARTS):
            wave[i][n].wait_recv()
            cross(part, step(part[3][2], 4 - k))
    for copy in codes_wave:
        copy.wait_recv()
    codes_core = push(t3.at[:, :, :, other_core], t4.at[me["c"]], c=other_core)
    t4[me["c"]] = t3[:, :, :, me["c"]]

    w_copy.wait()
    logits[...] = jnp.zeros_like(logits)

    def add_logits(c):
        @pl.loop(0, 4)
        def _(z):
            rows = h_all[c, z, :, :, :, pl.ds(0, CHUNK)].reshape(256, CHUNK)
            logits[...] += jnp.dot(rows, w_all[c * 4 + z], preferred_element_type=F32)

    add_logits(me["c"])
    for copy in crossing:
        copy.wait_recv()
    add_logits(other_core)
    h_copy = local(h_all.at[:, :, :, :, :, pl.ds(0, CHUNK)], h_out)

    codes_core.wait_recv()
    block = lax.broadcasted_iota(jnp.int32, (128, 512), 0)
    column = lax.broadcasted_iota(jnp.int32, (128, 512), 1)
    pick = (block == vo * 4 + column // 128).astype(F32).astype(BF16)
    scale = jnp.dot(
        h_all[0, dp, :, :, :, pl.ds(CHUNK, 128)].reshape(256, 128), pick, preferred_element_type=F32
    )
    for x in range(4):
        for y in range(4):
            row = (x * 4 + y) * 16
            code = jnp.concatenate(
                [t4[c, z, y, x].astype(F32) for z in range(4) for c in range(2)], axis=0
            )
            teacher[pl.ds(row, 16), :] = code * scale[row : row + 16]

    lg, tc = logits[...], teacher[...]
    first = (dp * 32 + vo) * 512
    hit = (first + lax.broadcasted_iota(jnp.int32, (256, 512), 1)) == tgt_in[...]
    m_s = jnp.max(lg, axis=1, keepdims=True)
    m_t = jnp.max(tc, axis=1, keepdims=True)
    w_t = jnp.exp(tc - m_t)
    stats = (
        m_s, jnp.sum(jnp.exp(lg - m_s), axis=1, keepdims=True),
        m_t, jnp.sum(w_t, axis=1, keepdims=True),
        jnp.sum(w_t * (tc - lg), axis=1, keepdims=True),
        jnp.sum(jnp.where(hit, lg, 0.0), axis=1, keepdims=True),
    )
    lane = lax.broadcasted_iota(jnp.int32, (256, 128), 1)
    packed = jnp.zeros((256, 128), F32)
    for n, value in enumerate(stats):
        packed = jnp.where(lane == n, value, packed)
    mine = packed.T[:8]

    def merge(parts):
        m1 = functools.reduce(jnp.maximum, [p[0:1] for p in parts])
        m2 = functools.reduce(jnp.maximum, [p[2:3] for p in parts])
        e1 = [jnp.exp(p[0:1] - m1) for p in parts]
        e2 = [jnp.exp(p[2:3] - m2) for p in parts]
        s1 = sum(p[1:2] * e for p, e in zip(parts, e1))
        s2 = sum(p[3:4] * e for p, e in zip(parts, e2))
        cross_sum = sum(p[4:5] * e for p, e in zip(parts, e2))
        target = sum(p[5:6] for p in parts)
        pad = jnp.zeros((2, 256), F32)
        return jnp.concatenate([m1, s1, m2, s2, cross_sum, target, pad], axis=0)

    for axis, slots in (("c", st_core), ("x", st_x), ("y", st_y), ("z", st_z)):
        size = slots.shape[0]
        slots[0] = mine
        copies = [
            push(slots.at[0], slots.at[k], **{axis: step(axis, k)}) for k in ((1,) if size == 2 else (1, 3, 2))
        ]
        for copy in copies:
            copy.wait_recv()
        mine = merge([slots[k] for k in range(size)])

    log_s = mine[0:1] + jnp.log(mine[1:2])
    log_t = mine[2:3] + jnp.log(mine[3:4])
    loss = mine[4:5] / mine[3:4] - log_t + log_s + CE_WEIGHT * (log_s - mine[5:6])
    loss_out[...] = jnp.broadcast_to(loss, (8, 256))
    columns = jnp.concatenate([log_s, log_t, jnp.zeros((126, 256), F32)], axis=0).T
    grad = GRAD_SCALE * (
        (1.0 + CE_WEIGHT) * jnp.exp(logits[...] - columns[:, 0:1])
        - jnp.exp(teacher[...] - columns[:, 1:2])
        - CE_WEIGHT * hit.astype(F32)
    )
    grad_out[...] = grad.astype(BF16)

    def partial_of(c, z):
        return lax.dot_general(
            grad_out[...], w_all[c * 4 + z], (((1,), (1,)), ((), ())), preferred_element_type=F32
        ).reshape(4, 4, 16, CHUNK)

    crossing = []
    for z in range(4):
        send_c[z] = partial_of(other_core, z).astype(BF16)
        crossing.append(push(send_c.at[z], recv_c.at[z], c=other_core))

    @pl.loop(0, 4)
    def _(z):
        own[z] = partial_of(me["c"], z)

    for copy in crossing:
        copy.wait_recv()

    @pl.loop(0, 4)
    def _(z):
        total = own[z] + recv_c[z].astype(F32)
        own[z] = total
        summed[z] = total.astype(BF16)

    r3, f2, b2 = (r3a, r3b, r3c), (f2a, f2b, f2c), (b2a, b2b, b2c)
    r2, f1, r1 = (r2a, r2b, r2c), (f1a, f1b, f1c), (r1a, r1b, r1c)

    def at_axis(axes, axis, coordinate):
        return tuple(coordinate if a == axis else slice(None) for a in axes)

    waves = []
    for i, part in enumerate(PARTS):
        axis, cols = part[3][2], pl.ds(part[0], part[2])
        waves.append([
            push(summed.at[(*at_axis("zxy", axis, step(axis, k)), slice(None), cols)], r3[i].at[k - 1], **{axis: step(axis, k)})
            for k in (1, 3, 2)
        ])
    for i, part in enumerate(PARTS):
        axis, cols = part[3][2], pl.ds(part[0], part[2])
        for copy in waves[i]:
            copy.wait_recv()
        total = own[(*at_axis("zxy", axis, me[axis]), slice(None), cols)]
        for k in range(3):
            total = total + r3[i][k].astype(F32)
        f2[i][...] = total
        b2[i][...] = total.astype(BF16)
        rest = "zxy".replace(axis, "")
        axis = part[3][1]
        waves[i] = [
            push(b2[i].at[at_axis(rest, axis, step(axis, k))], r2[i].at[k - 1], **{axis: step(axis, k)})
            for k in (1, 3, 2)
        ]
    for i, part in enumerate(PARTS):
        for copy in waves[i]:
            copy.wait_recv()
        rest = "zxy".replace(part[3][2], "")
        axis = part[3][1]
        total = f2[i][at_axis(rest, axis, me[axis])]
        for k in range(3):
            total = total + r2[i][k].astype(F32)
        f1[i][...] = total
        axis = part[3][0]
        waves[i] = [push(f1[i].at[step(axis, k)], r1[i].at[k - 1], **{axis: step(axis, k)}) for k in (1, 3, 2)]
    for i, part in enumerate(PARTS):
        for copy in waves[i]:
            copy.wait_recv()
        total = f1[i][me[part[3][0]]]
        for k in range(3):
            total = total + r1[i][k]
        for z in range(4):
            for c in range(2):
                row = (z * 2 + c) * 2
                fin_s[c, z, :, pl.ds(part[0], part[2])] = total[row : row + 2]

    arriving = []
    for k in range(4):
        for e in range(2):
            if (k, e) != (0, 0):
                z, c = step("z", k), step("c", e)
                arriving.append(push(fin_s.at[c, z], fin_r.at[me["c"], me["z"]], z=z, c=c))
    fin_r[me["c"], me["z"]] = fin_s[me["c"], me["z"]]
    for copy in arriving:
        copy.wait_recv()
    for c in range(2):
        for z in range(4):
            hg_out[:, pl.ds((c * 4 + z) * CHUNK, CHUNK)] = fin_r[c, z]

    h_copy.wait()
    for copy in unsent:
        copy.wait_send()


def head_kernel(h_ref, grad_ref, out_ref):
    out_ref[...] = lax.dot_general(
        h_ref[0], grad_ref[...], (((0,), (0,)), ((), ())), preferred_element_type=F32
    ).astype(BF16)


def per_device(hidden_states, head_weight, teacher_codes, teacher_scales, targets):
    codes = teacher_codes.reshape(2, 128, 512).transpose(1, 0, 2).reshape(2, 2, 4, 4, 2, 2, 512)
    weight = head_weight.reshape(8, CHUNK, 512)
    target = targets.reshape(2, 2, 4, 4, 2, 2).transpose(2, 0, 4, 3, 1, 5).reshape(256, 1)

    vmem = pltpu.VMEM
    scratch = [
        vmem((2, 4, 4, 4, 16, WIDE), BF16),
        vmem((8, CHUNK, 512), BF16),
        vmem((2, 4, 2, WIDE), BF16),
        vmem((2, 4, 2, WIDE), BF16),
        vmem((4, 2, 2, 4, 2, 2, 512), BF16),
        vmem((4, 4, 2, 4, 2, 512), BF16),
        vmem((4, 4, 4, 2, 2, 512), BF16),
        vmem((2, 4, 4, 4, 2, 512), BF16),
        vmem((256, 512), F32),
        vmem((256, 512), F32),
        vmem((2, 8, 256), F32),
        vmem((4, 8, 256), F32),
        vmem((4, 8, 256), F32),
        vmem((4, 8, 256), F32),
        vmem((4, 4, 4, 16, CHUNK), F32),
        vmem((4, 4, 4, 16, CHUNK), BF16),
        vmem((4, 4, 4, 16, CHUNK), BF16),
        vmem((4, 4, 4, 16, CHUNK), BF16),
    ]
    widths = [part[2] for part in PARTS]
    scratch += [vmem((3, 4, 4, 16, n), BF16) for n in widths]
    scratch += [vmem((4, 4, 16, n), F32) for n in widths]
    scratch += [vmem((4, 4, 16, n), BF16) for n in widths]
    scratch += [vmem((3, 4, 16, n), BF16) for n in widths]
    scratch += [vmem((4, 16, n), F32) for n in widths]
    scratch += [vmem((3, 16, n), F32) for n in widths]
    scratch += [vmem((2, 4, 2, CHUNK), F32), vmem((2, 4, 2, CHUNK), F32)]
    scratch += [
        pltpu.SemaphoreType.DMA((112,)),
        pltpu.SemaphoreType.DMA((112,)),
        pltpu.SemaphoreType.DMA((20,)),
    ]
    hidden_grad, loss, grad, gathered = pl.pallas_call(
        kernel,
        out_shape=(
            jax.ShapeDtypeStruct((2, 8192), F32),
            jax.ShapeDtypeStruct((8, 256), F32),
            jax.ShapeDtypeStruct((256, 512), BF16),
            jax.ShapeDtypeStruct((2, 4, 4, 4, 16, CHUNK), BF16),
        ),
        in_specs=[pl.BlockSpec(memory_space=pl.ANY)] * 4 + [pl.BlockSpec(memory_space=pltpu.VMEM)],
        out_specs=[pl.BlockSpec(memory_space=pltpu.VMEM)] * 3 + [pl.BlockSpec(memory_space=pl.ANY)],
        scratch_shapes=scratch,
        compiler_params=pltpu.CompilerParams(
            collective_id=0, has_side_effects=True, vmem_limit_bytes=56 * 1024 * 1024
        ),
    )(hidden_states, weight, codes, teacher_scales, target)

    head_grad = pl.pallas_call(
        head_kernel,
        grid=(8,),
        out_shape=jax.ShapeDtypeStruct((8192, 512), BF16),
        in_specs=[
            pl.BlockSpec((1, 256, CHUNK), lambda g: (g, 0, 0)),
            pl.BlockSpec((256, 512), lambda g: (0, 0)),
        ],
        out_specs=pl.BlockSpec((CHUNK, 512), lambda g: (g, 0)),
        compiler_params=pltpu.CompilerParams(vmem_limit_bytes=32 * 1024 * 1024),
    )(gathered.reshape(8, 256, CHUNK), grad)

    token_loss = loss[0].reshape(4, 2, 2, 4, 2, 2).transpose(1, 4, 0, 3, 2, 5).reshape(256)
    return hidden_grad, head_grad, token_loss


def solution(mesh):
    return jax.shard_map(
        per_device,
        mesh=mesh,
        in_specs=(
            P(AXES, None),
            P(None, AXES),
            P(AXES, None),
            P(AXES, None),
            P(),
        ),
        out_specs=(P(AXES, None), P(None, AXES), P()),
        check_vma=False,
    )
```

```python
import functools

import jax
import jax.numpy as jnp
from jax import lax
from jax.experimental import pallas as pl
from jax.experimental.pallas import tpu as pltpu
from jax.sharding import PartitionSpec as P

GRAD_SCALE = 32.0
CE_WEIGHT = 0.5
F32, BF16 = jnp.float32, jnp.bfloat16
MESH = pl.DeviceIdType.MESH
AXES = ("dp", "vocab")

CHUNK = 1024
WIDE = CHUNK + 128
PARTS = (
    (0, 384, 384, "xyz"),
    (384, 384, 384, "yzx"),
    (768, 384, 256, "zxy"),
)


Z_ORDER = (2, 1, 3, 0)


def kernel(
    h_in, w_in, codes_in, scales_in, tgt_in,
    hg_out, loss_out, grad_out, ht_out,
    h_all, w_all, src8, pre8, t1, t2, t3, t4, logits, teacher, grad_v, ht_v,
    st_a, st_b, own, send_c, recv_c, summed,
    fl_a, fl_b, fl_c, fr_a, fr_b, fr_c, rl_a, rl_b, rl_c, rr_a, rr_b, rr_c,
    f2a, f2b, f2c, b2a, b2b, b2c, r2a, r2b, r2c,
    f1a, f1b, f1c, r1a, r1b, r1c, fin_s, fin_r, loss_v,
    send_sems, recv_sems, local_sems,
):
    dp, vo = lax.axis_index("dp"), lax.axis_index("vocab")
    me = {"x": vo // 8, "z": (vo // 2) % 4, "y": (dp // 2) * 2 + vo % 2, "c": dp % 2}

    def device(**other):
        at = {**me, **other}
        return ((at["y"] // 2) * 2 + at["c"], (at["x"] * 4 + at["z"]) * 2 + at["y"] % 2)

    def step(axis, k):
        return lax.rem(me[axis] + k, 2 if axis == "c" else 4)

    count = {"remote": 0, "local": 0}
    unsent, unstored = [], []

    def push(src, dst, **other):
        n = count["remote"]
        count["remote"] += 1
        copy = pltpu.make_async_remote_copy(
            src_ref=src, dst_ref=dst, send_sem=send_sems.at[n], recv_sem=recv_sems.at[n],
            device_id=device(**other), device_id_type=MESH,
        )
        copy.start()
        unsent.append(copy)
        return copy

    def local(src, dst):
        n = count["local"]
        count["local"] += 1
        copy = pltpu.make_async_copy(src, dst, local_sems.at[n])
        copy.start()
        return copy

    barrier = pltpu.get_barrier_semaphore()
    partners = [dict(x=step("x", i), y=step("y", k)) for i in range(4) for k in range(4) if (i, k) != (0, 0)]
    group = [(k, e) for k in range(4) for e in range(2) if (k, e) != (0, 0)]
    partners += [dict(z=step("z", k), c=step("c", e)) for k, e in group]
    for other in partners:
        pl.semaphore_signal(barrier, inc=1, device_id=device(**other), device_id_type=MESH)

    heads = [local(h_in, src8.at[:, :, :, pl.ds(0, CHUNK)])]
    heads += [local(scales_in, src8.at[c, :, :, pl.ds(CHUNK, 128)]) for c in range(2)]
    own_codes = local(codes_in.at[:, :, me["x"]], t1.at[me["x"]])
    w_copy = local(w_in, w_all)
    for copy in heads:
        copy.wait()
    pl.semaphore_wait(barrier, len(partners))

    arriving = []
    for k, e in group:
        z, c = step("z", k), step("c", e)
        arriving.append(push(src8.at[c, z], pre8.at[me["c"], me["z"]], z=z, c=c))
    pre8[me["c"], me["z"]] = src8[me["c"], me["z"]]
    k_row = lax.broadcasted_iota(jnp.int32, (256, 256), 0)
    n_col = lax.broadcasted_iota(jnp.int32, (256, 256), 1)
    natural = (
        ((k_row >> 5) & 1) * 128 + ((k_row >> 1) & 1) * 64 + (k_row >> 6) * 16
        + ((k_row >> 2) & 3) * 4 + ((k_row >> 4) & 1) * 2 + (k_row & 1)
    )
    reorder = natural == n_col
    target = jnp.sum(jnp.where(reorder, tgt_in[...].astype(F32), 0.0), axis=1, keepdims=True)
    first = (dp * 32 + vo) * 512
    hit = (first + lax.broadcasted_iota(jnp.int32, (256, 512), 1)).astype(F32) == target
    for copy in arriving:
        copy.wait_recv()
    h_all[me["c"], me["z"], me["x"], me["y"]] = jnp.concatenate(
        [pre8[c, z].astype(F32) for z in range(4) for c in range(2)], axis=0
    ).astype(BF16)

    def gathered(part, free, half=None, **fixed):
        at = {**me, **fixed}
        index, halved = [], half is None
        for a in "zxy":
            if a not in free:
                index.append(at[a])
            elif halved:
                index.append(slice(None))
            else:
                index.append(pl.ds(half * 2, 2))
                halved = True
        return h_all.at[(me["c"], *index, slice(None), pl.ds(part[0], part[1]))]

    def gather_phase(part, p):
        order = part[3]
        view = gathered(part, order[:p])
        axis = order[p]
        return [push(view, view, **{axis: step(axis, k)}) for k in (2, 1, 3)]

    wave = [gather_phase(part, 0) for part in PARTS]
    codes_wave = [push(codes_in.at[:, :, step("x", k)], t1.at[me["x"]], x=step("x", k)) for k in (2, 1, 3)]
    for i, part in enumerate(PARTS):
        for copy in wave[i]:
            copy.wait_recv()
        wave[i] = gather_phase(part, 1)
    for copy in codes_wave:
        copy.wait_recv()
    own_codes.wait()
    codes_wave = [
        push(t1.at[:, step("y", k) // 2, :, :, step("y", k) % 2], t2.at[me["y"]], y=step("y", k))
        for k in (2, 1, 3)
    ]
    t2[me["y"]] = t1[:, me["y"] // 2, :, :, me["y"] % 2]

    other_core = step("c", 1)
    crossing, right, left = [], [], []

    def ring(part, coordinate, half, k):
        axis = part[3][2]
        view = gathered(part, part[3][:2], half, **{axis: coordinate})
        return push(view, view, **{axis: step(axis, k)})

    def cross(part, coordinate, half=None):
        view = gathered(part, part[3][:2], half, **{part[3][2]: coordinate})
        crossing.append(push(view, view, c=other_core))

    for i, part in enumerate(PARTS):
        for copy in wave[i]:
            copy.wait_recv()
        here = me[part[3][2]]
        up0, down1 = ring(part, here, 0, 1), ring(part, here, 1, 3)
        right.append([up0, ring(part, here, 1, 1)])
        left.append([ring(part, here, 0, 3), down1])
    for part in PARTS:
        cross(part, me[part[3][2]])
    forward = []
    for i, part in enumerate(PARTS):
        right[i][0].wait_recv()
        up = ring(part, step(part[3][2], 3), 0, 1)
        left[i][1].wait_recv()
        forward.append((up, ring(part, step(part[3][2], 1), 1, 3)))
    for copy in codes_wave:
        copy.wait_recv()
    codes_wave = [push(t2.at[:, :, :, step("z", k)], t3.at[me["z"]], z=step("z", k)) for k in (2, 1, 3)]
    t3[me["z"]] = t2[:, :, :, me["z"]]
    for i, part in enumerate(PARTS):
        right[i][1].wait_recv()
        cross(part, step(part[3][2], 3))
        left[i][0].wait_recv()
        cross(part, step(part[3][2], 1))
    for i, part in enumerate(PARTS):
        forward[i][0].wait_recv()
        cross(part, step(part[3][2], 2), 0)
        forward[i][1].wait_recv()
        cross(part, step(part[3][2], 2), 1)
    for copy in codes_wave:
        copy.wait_recv()
    codes_core = push(t3.at[:, :, :, other_core], t4.at[me["c"]], c=other_core)
    t4[me["c"]] = t3[:, :, :, me["c"]]

    w_copy.wait()
    logits[...] = jnp.zeros_like(logits)

    def add_logits(c):
        @pl.loop(0, 4)
        def _(z):
            rows = h_all[c, z, :, :, :, pl.ds(0, CHUNK)].reshape(256, CHUNK)
            logits[...] += jnp.dot(rows, w_all[c * 4 + z], preferred_element_type=F32)

    add_logits(me["c"])
    block = lax.broadcasted_iota(jnp.int32, (128, 512), 0)
    column = lax.broadcasted_iota(jnp.int32, (128, 512), 1)
    pick = (block == vo * 4 + column // 128).astype(F32).astype(BF16)
    scale = jnp.dot(
        h_all[me["c"], dp, :, :, :, pl.ds(CHUNK, 128)].reshape(256, 128), pick, preferred_element_type=F32
    )
    codes_core.wait_recv()
    for x in range(4):
        for y in range(4):
            row = (x * 4 + y) * 16
            code = jnp.concatenate(
                [t4[c, z, y, x].astype(F32) for z in range(4) for c in range(2)], axis=0
            )
            teacher[pl.ds(row, 16), :] = code * scale[row : row + 16]
    for copy in crossing:
        copy.wait_recv()
    add_logits(other_core)

    lg, tc = logits[...], teacher[...]
    m_s = jnp.max(lg, axis=1, keepdims=True)
    m_t = jnp.max(tc, axis=1, keepdims=True)
    w_t = jnp.exp(tc - m_t)
    stats = (
        m_s, jnp.sum(jnp.exp(lg - m_s), axis=1, keepdims=True),
        m_t, jnp.sum(w_t, axis=1, keepdims=True),
        jnp.sum(w_t * (tc - lg), axis=1, keepdims=True),
        jnp.sum(jnp.where(hit, lg, 0.0), axis=1, keepdims=True),
    )
    lane = lax.broadcasted_iota(jnp.int32, (256, 128), 1)
    packed = jnp.zeros((256, 128), F32)
    for n, value in enumerate(stats):
        packed = jnp.where(lane == n, value, packed)
    mine = packed.T[:8]

    def merge(parts):
        m1 = functools.reduce(jnp.maximum, [p[0:1] for p in parts])
        m2 = functools.reduce(jnp.maximum, [p[2:3] for p in parts])
        e1 = [jnp.exp(p[0:1] - m1) for p in parts]
        e2 = [jnp.exp(p[2:3] - m2) for p in parts]
        s1 = sum(p[1:2] * e for p, e in zip(parts, e1))
        s2 = sum(p[3:4] * e for p, e in zip(parts, e2))
        cross_sum = sum(p[4:5] * e for p, e in zip(parts, e2))
        target = sum(p[5:6] for p in parts)
        pad = jnp.zeros((2, 256), F32)
        return jnp.concatenate([m1, s1, m2, s2, cross_sum, target, pad], axis=0)

    def transpose_chunks(c):
        @pl.loop(0, 4)
        def _(z):
            ht_v[c * 4 + z] = h_all[c, z, :, :, :, pl.ds(0, CHUNK)].reshape(256, CHUNK).T
        unstored.append(local(ht_v.at[pl.ds(c * 4, 4)], ht_out.at[pl.ds(c * 4, 4)]))

    st_a[0] = mine
    copies = [
        push(st_a.at[0], st_a.at[1 + n], z=step("z", k), c=step("c", e)) for n, (k, e) in enumerate(group)
    ]
    transpose_chunks(0)
    for copy in copies:
        copy.wait_recv()
    mine = merge([st_a[k] for k in range(8)])
    st_b[0] = mine
    pairs = [(i, k) for i in range(4) for k in range(4) if (i, k) != (0, 0)]
    copies = [
        push(st_b.at[0], st_b.at[1 + n], x=step("x", i), y=step("y", k)) for n, (i, k) in enumerate(pairs)
    ]
    transpose_chunks(1)
    for copy in copies:
        copy.wait_recv()
    mine = merge([st_b[k] for k in range(16)])

    log_s = mine[0:1] + jnp.log(mine[1:2])
    log_t = mine[2:3] + jnp.log(mine[3:4])
    loss = mine[4:5] / mine[3:4] - log_t + log_s + CE_WEIGHT * (log_s - mine[5:6])
    columns = jnp.concatenate([log_s, log_t, loss, jnp.zeros((125, 256), F32)], axis=0).T
    grad = GRAD_SCALE * (
        (1.0 + CE_WEIGHT) * jnp.exp(logits[...] - columns[:, 0:1])
        - jnp.exp(teacher[...] - columns[:, 1:2])
        - CE_WEIGHT * hit.astype(F32)
    )
    grad_v[...] = grad.astype(BF16)
    unstored.append(local(grad_v, grad_out))

    def partial_of(c, j):
        return lax.dot_general(
            grad_v[...], w_all[c * 4 + step("z", Z_ORDER[j])], (((1,), (1,)), ((), ())), preferred_element_type=F32
        ).reshape(4, 4, 16, CHUNK)

    crossing = []

    def send_partial(j):
        send_c[j] = partial_of(other_core, j).astype(BF16)
        crossing.append(push(send_c.at[j], recv_c.at[j], c=other_core))

    fl, fr, rl, rr = (fl_a, fl_b, fl_c), (fr_a, fr_b, fr_c), (rl_a, rl_b, rl_c), (rr_a, rr_b, rr_c)
    f2, b2 = (f2a, f2b, f2c), (b2a, b2b, b2c)
    r2, f1, r1 = (r2a, r2b, r2c), (f1a, f1b, f1c), (r1a, r1b, r1c)
    half0, half1 = two = pl.ds(0, 2), pl.ds(2, 2)
    ring_waits = {}

    def block_of(i, k, j, half):
        cols = pl.ds(PARTS[i][0], PARTS[i][2])
        if i == 0:
            return (Z_ORDER.index(k), slice(None), half, slice(None), cols)
        if i == 1:
            return (two[j], step("x", k), half, slice(None), cols)
        return (two[j], half, step("y", k), slice(None), cols)

    def landing(i, j, half):
        return (slice(None), half) if i == 0 else (j, slice(None), half)

    def ring_push(i, k, j, half, buffer, toward):
        axis = PARTS[i][3][2]
        if buffer is fl or buffer is fr:
            place = slice(None) if i == 0 else j
        else:
            place = landing(i, j, half)
        return push(
            summed.at[block_of(i, k, j, half)], buffer[i].at[place], **{axis: step(axis, toward)}
        )

    def ring_opposite(i, j):
        ring_waits[i, j] = [ring_push(i, 2, j, half0, fl, 1), ring_push(i, 2, j, half1, fr, 3)]

    def ring_up(i, j):
        ring_waits[i, j].append(ring_push(i, 1, j, half1, rl, 1))

    def ring_down(i, j):
        ring_waits[i, j].append(ring_push(i, 3, j, half0, rr, 3))

    def ring_forward(i, j):
        waits = ring_waits[i, j]
        place = slice(None) if i == 0 else j
        for n, (k, half, came, buffer) in enumerate(((1, half0, fl, rl), (3, half1, fr, rr))):
            waits[n].wait_recv()
            index = block_of(i, k, j, half)
            summed[index] = (own[index] + came[i][place].astype(F32)).astype(BF16)
            waits.append(ring_push(i, k, j, half, buffer, k))

    def add_chunk(j):
        crossing[j].wait_recv()
        total = own[j] + recv_c[j].astype(F32)
        own[j] = total
        summed[j] = total.astype(BF16)

    send_partial(0)
    send_partial(1)
    own[0] = partial_of(me["c"], 0)
    add_chunk(0)
    ring_opposite(0, 0)
    send_partial(2)
    own[1] = partial_of(me["c"], 1)
    add_chunk(1)
    ring_opposite(1, 0)
    ring_opposite(2, 0)
    ring_up(0, 0)
    for i in (1, 2):
        ring_up(i, 0)
        ring_down(i, 0)
    send_partial(3)
    own[2] = partial_of(me["c"], 2)
    add_chunk(2)
    ring_down(0, 0)
    ring_forward(0, 0)
    own[3] = partial_of(me["c"], 3)
    add_chunk(3)
    ring_opposite(1, 1)
    ring_opposite(2, 1)
    for i in (1, 2):
        ring_up(i, 1)
        ring_down(i, 1)
    ring_forward(1, 0)
    ring_forward(2, 0)
    ring_forward(1, 1)
    ring_forward(2, 1)

    def at_axis(axes, axis, coordinate):
        return tuple(coordinate if a == axis else slice(None) for a in axes)

    waves = [None] * 3
    for i, part in enumerate(PARTS):
        for j in range(1 if i == 0 else 2):
            for copy in ring_waits[i, j][2:]:
                copy.wait_recv()
        axis, cols = part[3][2], pl.ds(part[0], part[2])
        mine_at = 3 if axis == "z" else me[axis]
        total = own[(*at_axis("zxy", axis, mine_at), slice(None), cols)]
        total = total + rl[i][...].reshape(total.shape).astype(F32) + rr[i][...].reshape(total.shape).astype(F32)
        f2[i][...] = total
        b2[i][...] = total.astype(BF16)
        rest = "zxy".replace(axis, "")
        axis = part[3][1]
        waves[i] = [
            push(
                b2[i].at[at_axis(rest, axis, Z_ORDER.index(k) if axis == "z" else step(axis, k))],
                r2[i].at[k - 1], **{axis: step(axis, k)},
            )
            for k in (2, 1, 3)
        ]
    for i, part in enumerate(PARTS):
        for copy in waves[i]:
            copy.wait_recv()
        rest = "zxy".replace(part[3][2], "")
        axis = part[3][1]
        total = f2[i][at_axis(rest, axis, 3 if axis == "z" else me[axis])]
        for k in range(3):
            total = total + r2[i][k].astype(F32)
        f1[i][...] = total
        axis = part[3][0]
        waves[i] = [
            push(
                f1[i].at[Z_ORDER.index(k) if axis == "z" else step(axis, k)], r1[i].at[k - 1],
                **{axis: step(axis, k)},
            )
            for k in (2, 1, 3)
        ]
    loss_v[...] = jnp.broadcast_to(
        jnp.sum(jnp.where(reorder, columns[:, 2:3], 0.0), axis=0, keepdims=True), (8, 256)
    )
    unstored.append(local(loss_v, loss_out))
    for i, part in enumerate(PARTS):
        for copy in waves[i]:
            copy.wait_recv()
        total = f1[i][3 if part[3][0] == "z" else me[part[3][0]]]
        for k in range(3):
            total = total + r1[i][k]
        for z in range(4):
            for c in range(2):
                row = (z * 2 + c) * 2
                fin_s[c, z, :, pl.ds(part[0], part[2])] = total[row : row + 2]

    arriving = []
    for k, e in group:
        z, c = step("z", k), step("c", e)
        arriving.append(push(fin_s.at[c, z], fin_r.at[me["c"], me["z"]], z=z, c=c))
    fin_r[me["c"], me["z"]] = fin_s[me["c"], me["z"]]
    for copy in arriving:
        copy.wait_recv()
    unstored.append(local(fin_r, hg_out))
    for copy in unsent:
        copy.wait_send()
    for copy in unstored:
        copy.wait()


def head_kernel(ht_ref, grad_ref, hg_ref, loss_ref, out_ref, hg_out, loss_out):
    out_ref[...] = jnp.dot(ht_ref[...], grad_ref[...], preferred_element_type=F32).astype(BF16)

    @pl.when(pl.program_id(0) == 0)
    def _():
        for g in range(8):
            hg_out[:, pl.ds(g * CHUNK, CHUNK)] = hg_ref[g]
        loss_out[...] = loss_ref[0]


def per_device(hidden_states, head_weight, teacher_codes, teacher_scales, targets):
    hidden = hidden_states.reshape(2, 8, CHUNK).transpose(1, 0, 2).reshape(2, 4, 2, CHUNK)
    scales = teacher_scales.reshape(2, 4, 128).transpose(1, 0, 2)
    codes = teacher_codes.reshape(2, 128, 512).transpose(1, 0, 2).reshape(2, 2, 4, 4, 2, 2, 512)
    weight = head_weight.reshape(8, CHUNK, 512)

    vmem = pltpu.VMEM
    scratch = [
        vmem((2, 4, 4, 4, 16, WIDE), BF16),
        vmem((8, CHUNK, 512), BF16),
        vmem((2, 4, 2, WIDE), BF16),
        vmem((2, 4, 2, WIDE), BF16),
        vmem((4, 2, 2, 4, 2, 2, 512), BF16),
        vmem((4, 4, 2, 4, 2, 512), BF16),
        vmem((4, 4, 4, 2, 2, 512), BF16),
        vmem((2, 4, 4, 4, 2, 512), BF16),
        vmem((256, 512), F32),
        vmem((256, 512), F32),
        vmem((256, 512), BF16),
        vmem((8, CHUNK, 256), BF16),
        vmem((8, 8, 256), F32),
        vmem((16, 8, 256), F32),
        vmem((4, 4, 4, 16, CHUNK), F32),
        vmem((4, 4, 4, 16, CHUNK), BF16),
        vmem((4, 4, 4, 16, CHUNK), BF16),
        vmem((4, 4, 4, 16, CHUNK), BF16),
    ]
    widths = [part[2] for part in PARTS]
    forwarded = [(4, 2, 16, widths[0]), (2, 2, 2, 16, widths[1]), (2, 2, 2, 16, widths[2])]
    arrived = [(4, 4, 16, widths[0]), (2, 2, 4, 16, widths[1]), (2, 2, 4, 16, widths[2])]
    scratch += [vmem(shape, BF16) for shape in forwarded * 2 + arrived * 2]
    scratch += [vmem((4, 4, 16, n), F32) for n in widths]
    scratch += [vmem((4, 4, 16, n), BF16) for n in widths]
    scratch += [vmem((3, 4, 16, n), BF16) for n in widths]
    scratch += [vmem((4, 16, n), F32) for n in widths]
    scratch += [vmem((3, 16, n), F32) for n in widths]
    scratch += [vmem((2, 4, 2, CHUNK), F32), vmem((2, 4, 2, CHUNK), F32), vmem((8, 256), F32)]
    scratch += [
        pltpu.SemaphoreType.DMA((176,)),
        pltpu.SemaphoreType.DMA((176,)),
        pltpu.SemaphoreType.DMA((16,)),
    ]
    hidden_grad, loss, grad, hidden_t = pl.pallas_call(
        kernel,
        out_shape=(
            jax.ShapeDtypeStruct((2, 4, 2, CHUNK), F32),
            jax.ShapeDtypeStruct((8, 256), F32),
            jax.ShapeDtypeStruct((256, 512), BF16),
            jax.ShapeDtypeStruct((8, CHUNK, 256), BF16),
        ),
        in_specs=[pl.BlockSpec(memory_space=pl.ANY)] * 4 + [pl.BlockSpec(memory_space=pltpu.VMEM)],
        out_specs=[pl.BlockSpec(memory_space=pl.ANY)] * 4,
        scratch_shapes=scratch,
        compiler_params=pltpu.CompilerParams(
            collective_id=0, has_side_effects=True, vmem_limit_bytes=60 * 1024 * 1024
        ),
    )(hidden, weight, codes, scales, targets.reshape(1, 256))

    head_grad, hidden_grad, token_loss = pl.pallas_call(
        head_kernel,
        grid=(8,),
        out_shape=(
            jax.ShapeDtypeStruct((8192, 512), BF16),
            jax.ShapeDtypeStruct((2, 8192), F32),
            jax.ShapeDtypeStruct((256,), F32),
        ),
        in_specs=[
            pl.BlockSpec((CHUNK, 256), lambda g: (g, 0)),
            pl.BlockSpec((256, 512), lambda g: (0, 0)),
            pl.BlockSpec((8, 2, CHUNK), lambda g: (0, 0, 0)),
            pl.BlockSpec((8, 256), lambda g: (0, 0)),
        ],
        out_specs=(
            pl.BlockSpec((CHUNK, 512), lambda g: (g, 0)),
            pl.BlockSpec((2, 8192), lambda g: (0, 0)),
            pl.BlockSpec((256,), lambda g: (0,)),
        ),
        compiler_params=pltpu.CompilerParams(vmem_limit_bytes=60 * 1024 * 1024),
    )(hidden_t.reshape(8192, 256), grad, hidden_grad.reshape(8, 2, CHUNK), loss)
    return hidden_grad, head_grad, token_loss


def solution(mesh):
    return jax.shard_map(
        per_device,
        mesh=mesh,
        in_specs=(
            P(AXES, None),
            P(None, AXES),
            P(AXES, None),
            P(AXES, None),
            P(),
        ),
        out_specs=(P(AXES, None), P(None, AXES), P()),
        check_vma=False,
    )
```

```python
import functools

import jax
import jax.numpy as jnp
from jax import lax
from jax.experimental import pallas as pl
from jax.experimental.pallas import tpu as pltpu
from jax.sharding import PartitionSpec as P

GRAD_SCALE = 32.0
CE_WEIGHT = 0.5
F32, BF16 = jnp.float32, jnp.bfloat16
MESH = pl.DeviceIdType.MESH
AXES = ("dp", "vocab")

CHUNK = 1024
WIDE = CHUNK + 128
PARTS = (
    (0, 384, 384, "xyz"),
    (384, 384, 384, "yzx"),
    (768, 384, 256, "zxy"),
)


Z_ORDER = (2, 1, 3, 0)


def kernel(
    h_in, w_in, codes_in, scales_in, tgt_in,
    hg_out, loss_out, grad_out, ht_out,
    h_all, w_all, src8, pre8, t1, t2, t3, t4, logits, teacher,
    st_a, st_b, own, send_c, recv_c, summed,
    fl_a, fl_b, fl_c, fr_a, fr_b, fr_c, rl_a, rl_b, rl_c, rr_a, rr_b, rr_c,
    f2a, f2b, f2c, b2a, b2b, b2c, r2a, r2b, r2c,
    f1a, f1b, f1c, r1a, r1b, r1c, fin_s, fin_r,
    send_sems, recv_sems, local_sems,
):
    dp, vo = lax.axis_index("dp"), lax.axis_index("vocab")
    me = {"x": vo // 8, "z": (vo // 2) % 4, "y": (dp // 2) * 2 + vo % 2, "c": dp % 2}

    def device(**other):
        at = {**me, **other}
        return ((at["y"] // 2) * 2 + at["c"], (at["x"] * 4 + at["z"]) * 2 + at["y"] % 2)

    def step(axis, k):
        return lax.rem(me[axis] + k, 2 if axis == "c" else 4)

    count = {"remote": 0, "local": 0}
    unsent = []

    def push(src, dst, **other):
        n = count["remote"]
        count["remote"] += 1
        copy = pltpu.make_async_remote_copy(
            src_ref=src, dst_ref=dst, send_sem=send_sems.at[n], recv_sem=recv_sems.at[n],
            device_id=device(**other), device_id_type=MESH,
        )
        copy.start()
        unsent.append(copy)
        return copy

    def local(src, dst):
        n = count["local"]
        count["local"] += 1
        copy = pltpu.make_async_copy(src, dst, local_sems.at[n])
        copy.start()
        return copy

    barrier = pltpu.get_barrier_semaphore()
    partners = [dict(x=step("x", i), y=step("y", k)) for i in range(4) for k in range(4) if (i, k) != (0, 0)]
    group = [(k, e) for k in range(4) for e in range(2) if (k, e) != (0, 0)]
    partners += [dict(z=step("z", k), c=step("c", e)) for k, e in group]
    for other in partners:
        pl.semaphore_signal(barrier, inc=1, device_id=device(**other), device_id_type=MESH)

    heads = [local(h_in, src8.at[:, :, :, pl.ds(0, CHUNK)])]
    heads += [local(scales_in, src8.at[c, :, :, pl.ds(CHUNK, 128)]) for c in range(2)]
    own_codes = local(codes_in.at[:, :, me["x"]], t1.at[me["x"]])
    w_copy = local(w_in, w_all)
    k_row = lax.broadcasted_iota(jnp.int32, (256, 256), 0)
    n_col = lax.broadcasted_iota(jnp.int32, (256, 256), 1)
    natural = (
        ((k_row >> 5) & 1) * 128 + ((k_row >> 1) & 1) * 64 + (k_row >> 6) * 16
        + ((k_row >> 2) & 3) * 4 + ((k_row >> 4) & 1) * 2 + (k_row & 1)
    )
    reorder = natural == n_col
    target = jnp.sum(jnp.where(reorder, tgt_in[...].astype(F32), 0.0), axis=1, keepdims=True)
    first = (dp * 32 + vo) * 512
    hit = (first + lax.broadcasted_iota(jnp.int32, (256, 512), 1)).astype(F32) == target
    for copy in heads:
        copy.wait()
    pl.semaphore_wait(barrier, len(partners))

    arriving = []
    for k, e in group:
        z, c = step("z", k), step("c", e)
        arriving.append(push(src8.at[c, z], pre8.at[me["c"], me["z"]], z=z, c=c))
    pre8[me["c"], me["z"]] = src8[me["c"], me["z"]]
    codes_wave = [push(codes_in.at[:, :, step("x", k)], t1.at[me["x"]], x=step("x", k)) for k in (2, 1, 3)]
    for copy in arriving:
        copy.wait_recv()
    h_all[me["c"], me["z"], me["x"], me["y"]] = jnp.concatenate(
        [pre8[c, z].astype(F32) for z in range(4) for c in range(2)], axis=0
    ).astype(BF16)

    def gathered(part, free, half=None, **fixed):
        at = {**me, **fixed}
        index, halved = [], half is None
        for a in "zxy":
            if a not in free:
                index.append(at[a])
            elif halved:
                index.append(slice(None))
            else:
                index.append(pl.ds(half * 2, 2))
                halved = True
        return h_all.at[(me["c"], *index, slice(None), pl.ds(part[0], part[1]))]

    def gather_phase(part, p):
        order = part[3]
        view = gathered(part, order[:p])
        axis = order[p]
        return [push(view, view, **{axis: step(axis, k)}) for k in (2, 1, 3)]

    wave = [gather_phase(part, 0) for part in PARTS]
    for copy in codes_wave:
        copy.wait_recv()
    own_codes.wait()
    codes_wave = [
        push(t1.at[:, step("y", k) // 2, :, :, step("y", k) % 2], t2.at[me["y"]], y=step("y", k))
        for k in (2, 1, 3)
    ]
    t2[me["y"]] = t1[:, me["y"] // 2, :, :, me["y"] % 2]
    for i, part in enumerate(PARTS):
        for copy in wave[i]:
            copy.wait_recv()
        wave[i] = gather_phase(part, 1)
    for copy in codes_wave:
        copy.wait_recv()
    codes_wave = [push(t2.at[:, :, :, step("z", k)], t3.at[me["z"]], z=step("z", k)) for k in (2, 1, 3)]
    t3[me["z"]] = t2[:, :, :, me["z"]]

    other_core = step("c", 1)
    crossing, right, left = [], [], []

    def ring(part, coordinate, half, k):
        axis = part[3][2]
        view = gathered(part, part[3][:2], half, **{axis: coordinate})
        return push(view, view, **{axis: step(axis, k)})

    def cross(part, coordinate, half=None):
        view = gathered(part, part[3][:2], half, **{part[3][2]: coordinate})
        crossing.append(push(view, view, c=other_core))

    for i, part in enumerate(PARTS):
        for copy in wave[i]:
            copy.wait_recv()
        here = me[part[3][2]]
        up0, down1 = ring(part, here, 0, 1), ring(part, here, 1, 3)
        right.append([up0, ring(part, here, 1, 1)])
        left.append([ring(part, here, 0, 3), down1])
    for part in PARTS:
        cross(part, me[part[3][2]])
    forward = []
    for i, part in enumerate(PARTS):
        right[i][0].wait_recv()
        up = ring(part, step(part[3][2], 3), 0, 1)
        left[i][1].wait_recv()
        forward.append((up, ring(part, step(part[3][2], 1), 1, 3)))
    for copy in codes_wave:
        copy.wait_recv()
    codes_core = push(t3.at[:, :, :, other_core], t4.at[me["c"]], c=other_core)
    t4[me["c"]] = t3[:, :, :, me["c"]]
    for i, part in enumerate(PARTS):
        right[i][1].wait_recv()
        cross(part, step(part[3][2], 3))
        left[i][0].wait_recv()
        cross(part, step(part[3][2], 1))
    for i, part in enumerate(PARTS):
        forward[i][0].wait_recv()
        cross(part, step(part[3][2], 2), 0)
        forward[i][1].wait_recv()
        cross(part, step(part[3][2], 2), 1)

    w_copy.wait()
    logits[...] = jnp.zeros_like(logits)

    def add_logits(c):
        @pl.loop(0, 4)
        def _(z):
            rows = h_all[c, z, :, :, :, pl.ds(0, CHUNK)].reshape(256, CHUNK)
            logits[...] += jnp.dot(rows, w_all[c * 4 + z], preferred_element_type=F32)

    add_logits(me["c"])
    block = lax.broadcasted_iota(jnp.int32, (128, 512), 0)
    column = lax.broadcasted_iota(jnp.int32, (128, 512), 1)
    pick = (block == vo * 4 + column // 128).astype(F32).astype(BF16)
    scale = jnp.dot(
        h_all[me["c"], dp, :, :, :, pl.ds(CHUNK, 128)].reshape(256, 128), pick, preferred_element_type=F32
    )
    codes_core.wait_recv()
    for x in range(4):
        for y in range(4):
            row = (x * 4 + y) * 16
            code = jnp.concatenate(
                [t4[c, z, y, x].astype(F32) for z in range(4) for c in range(2)], axis=0
            )
            teacher[pl.ds(row, 16), :] = code * scale[row : row + 16]
    for copy in crossing:
        copy.wait_recv()
    add_logits(other_core)

    lg, tc = logits[...], teacher[...]
    m_s = jnp.max(lg, axis=1, keepdims=True)
    m_t = jnp.max(tc, axis=1, keepdims=True)
    w_t = jnp.exp(tc - m_t)
    stats = (
        m_s, jnp.sum(jnp.exp(lg - m_s), axis=1, keepdims=True),
        m_t, jnp.sum(w_t, axis=1, keepdims=True),
        jnp.sum(w_t * (tc - lg), axis=1, keepdims=True),
        jnp.sum(jnp.where(hit, lg, 0.0), axis=1, keepdims=True),
    )
    lane = lax.broadcasted_iota(jnp.int32, (256, 128), 1)
    packed = jnp.zeros((256, 128), F32)
    for n, value in enumerate(stats):
        packed = jnp.where(lane == n, value, packed)
    mine = packed.T[:8]

    def merge(parts):
        m1 = functools.reduce(jnp.maximum, [p[0:1] for p in parts])
        m2 = functools.reduce(jnp.maximum, [p[2:3] for p in parts])
        e1 = [jnp.exp(p[0:1] - m1) for p in parts]
        e2 = [jnp.exp(p[2:3] - m2) for p in parts]
        s1 = sum(p[1:2] * e for p, e in zip(parts, e1))
        s2 = sum(p[3:4] * e for p, e in zip(parts, e2))
        cross_sum = sum(p[4:5] * e for p, e in zip(parts, e2))
        target = sum(p[5:6] for p in parts)
        pad = jnp.zeros((2, 256), F32)
        return jnp.concatenate([m1, s1, m2, s2, cross_sum, target, pad], axis=0)

    def transpose_chunks(c):
        @pl.loop(0, 4)
        def _(z):
            ht_out[c * 4 + z] = h_all[c, z, :, :, :, pl.ds(0, CHUNK)].reshape(256, CHUNK).T

    st_a[0] = mine
    copies = [
        push(st_a.at[0], st_a.at[1 + n], z=step("z", k), c=step("c", e)) for n, (k, e) in enumerate(group)
    ]
    transpose_chunks(0)
    for copy in copies:
        copy.wait_recv()
    mine = merge([st_a[k] for k in range(8)])
    st_b[0] = mine
    pairs = [(i, k) for i in range(4) for k in range(4) if (i, k) != (0, 0)]
    copies = [
        push(st_b.at[0], st_b.at[1 + n], x=step("x", i), y=step("y", k)) for n, (i, k) in enumerate(pairs)
    ]
    transpose_chunks(1)
    for copy in copies:
        copy.wait_recv()
    mine = merge([st_b[k] for k in range(16)])

    log_s = mine[0:1] + jnp.log(mine[1:2])
    log_t = mine[2:3] + jnp.log(mine[3:4])
    loss = mine[4:5] / mine[3:4] - log_t + log_s + CE_WEIGHT * (log_s - mine[5:6])
    columns = jnp.concatenate([log_s, log_t, loss, jnp.zeros((125, 256), F32)], axis=0).T
    grad = GRAD_SCALE * (
        (1.0 + CE_WEIGHT) * jnp.exp(logits[...] - columns[:, 0:1])
        - jnp.exp(teacher[...] - columns[:, 1:2])
        - CE_WEIGHT * hit.astype(F32)
    )
    grad_out[...] = grad.astype(BF16)

    def partial_of(c, j):
        return lax.dot_general(
            grad_out[...], w_all[c * 4 + step("z", Z_ORDER[j])], (((1,), (1,)), ((), ())), preferred_element_type=F32
        ).reshape(4, 4, 16, CHUNK)

    crossing = []

    def send_partial(j):
        send_c[j] = partial_of(other_core, j).astype(BF16)
        crossing.append(push(send_c.at[j], recv_c.at[j], c=other_core))

    fl, fr, rl, rr = (fl_a, fl_b, fl_c), (fr_a, fr_b, fr_c), (rl_a, rl_b, rl_c), (rr_a, rr_b, rr_c)
    f2, b2 = (f2a, f2b, f2c), (b2a, b2b, b2c)
    r2, f1, r1 = (r2a, r2b, r2c), (f1a, f1b, f1c), (r1a, r1b, r1c)
    half0, half1 = two = pl.ds(0, 2), pl.ds(2, 2)
    ring_waits = {}

    def block_of(i, k, j, half):
        cols = pl.ds(PARTS[i][0], PARTS[i][2])
        if i == 0:
            return (Z_ORDER.index(k), slice(None), half, slice(None), cols)
        if i == 1:
            return (two[j], step("x", k), half, slice(None), cols)
        return (two[j], half, step("y", k), slice(None), cols)

    def landing(i, j, half):
        return (slice(None), half) if i == 0 else (j, slice(None), half)

    def ring_push(i, k, j, half, buffer, toward):
        axis = PARTS[i][3][2]
        if buffer is fl or buffer is fr:
            place = slice(None) if i == 0 else j
        else:
            place = landing(i, j, half)
        return push(
            summed.at[block_of(i, k, j, half)], buffer[i].at[place], **{axis: step(axis, toward)}
        )

    def ring_opposite(i, j):
        ring_waits[i, j] = [ring_push(i, 2, j, half0, fl, 1), ring_push(i, 2, j, half1, fr, 3)]

    def ring_up(i, j):
        ring_waits[i, j].append(ring_push(i, 1, j, half1, rl, 1))

    def ring_down(i, j):
        ring_waits[i, j].append(ring_push(i, 3, j, half0, rr, 3))

    def ring_forward(i, j):
        waits = ring_waits[i, j]
        place = slice(None) if i == 0 else j
        for n, (k, half, came, buffer) in enumerate(((1, half0, fl, rl), (3, half1, fr, rr))):
            waits[n].wait_recv()
            index = block_of(i, k, j, half)
            summed[index] = (own[index] + came[i][place].astype(F32)).astype(BF16)
            waits.append(ring_push(i, k, j, half, buffer, k))

    def add_chunk(j):
        crossing[j].wait_recv()
        total = own[j] + recv_c[j].astype(F32)
        own[j] = total
        summed[j] = total.astype(BF16)

    send_partial(0)
    send_partial(1)
    own[0] = partial_of(me["c"], 0)
    add_chunk(0)
    ring_opposite(0, 0)
    send_partial(2)
    own[1] = partial_of(me["c"], 1)
    add_chunk(1)
    ring_opposite(1, 0)
    ring_opposite(2, 0)
    ring_up(0, 0)
    for i in (1, 2):
        ring_up(i, 0)
        ring_down(i, 0)
    send_partial(3)
    own[2] = partial_of(me["c"], 2)
    add_chunk(2)
    ring_down(0, 0)
    ring_forward(0, 0)
    own[3] = partial_of(me["c"], 3)
    add_chunk(3)
    ring_opposite(1, 1)
    ring_opposite(2, 1)
    for i in (1, 2):
        ring_up(i, 1)
        ring_down(i, 1)
    ring_forward(1, 0)
    ring_forward(2, 0)
    ring_forward(1, 1)
    ring_forward(2, 1)

    def at_axis(axes, axis, coordinate):
        return tuple(coordinate if a == axis else slice(None) for a in axes)

    waves = [None] * 3
    for i, part in enumerate(PARTS):
        for j in range(1 if i == 0 else 2):
            for copy in ring_waits[i, j][2:]:
                copy.wait_recv()
        axis, cols = part[3][2], pl.ds(part[0], part[2])
        mine_at = 3 if axis == "z" else me[axis]
        total = own[(*at_axis("zxy", axis, mine_at), slice(None), cols)]
        total = total + rl[i][...].reshape(total.shape).astype(F32) + rr[i][...].reshape(total.shape).astype(F32)
        f2[i][...] = total
        b2[i][...] = total.astype(BF16)
        rest = "zxy".replace(axis, "")
        axis = part[3][1]
        waves[i] = [
            push(
                b2[i].at[at_axis(rest, axis, Z_ORDER.index(k) if axis == "z" else step(axis, k))],
                r2[i].at[k - 1], **{axis: step(axis, k)},
            )
            for k in (2, 1, 3)
        ]
    for i, part in enumerate(PARTS):
        for copy in waves[i]:
            copy.wait_recv()
        rest = "zxy".replace(part[3][2], "")
        axis = part[3][1]
        total = f2[i][at_axis(rest, axis, 3 if axis == "z" else me[axis])]
        for k in range(3):
            total = total + r2[i][k].astype(F32)
        f1[i][...] = total
        axis = part[3][0]
        waves[i] = [
            push(
                f1[i].at[Z_ORDER.index(k) if axis == "z" else step(axis, k)], r1[i].at[k - 1],
                **{axis: step(axis, k)},
            )
            for k in (2, 1, 3)
        ]
    loss_out[...] = jnp.broadcast_to(
        jnp.sum(jnp.where(reorder, columns[:, 2:3], 0.0), axis=0, keepdims=True), (8, 256)
    )
    for i, part in enumerate(PARTS):
        for copy in waves[i]:
            copy.wait_recv()
        total = f1[i][3 if part[3][0] == "z" else me[part[3][0]]]
        for k in range(3):
            total = total + r1[i][k]
        for z in range(4):
            for c in range(2):
                row = (z * 2 + c) * 2
                fin_s[c, z, :, pl.ds(part[0], part[2])] = total[row : row + 2]

    arriving = []
    for k, e in group:
        z, c = step("z", k), step("c", e)
        arriving.append(push(fin_s.at[c, z], fin_r.at[me["c"], me["z"]], z=z, c=c))
    fin_r[me["c"], me["z"]] = fin_s[me["c"], me["z"]]
    for copy in arriving:
        copy.wait_recv()
    hg_out[...] = fin_r[...]
    for copy in unsent:
        copy.wait_send()


def head_kernel(ht_ref, grad_ref, hg_ref, loss_ref, out_ref, hg_out, loss_out, out_v, sems):
    copies = []
    for g in range(8):
        out_v[g] = jnp.dot(ht_ref[g], grad_ref[...], preferred_element_type=F32).astype(BF16)
        copy = pltpu.make_async_copy(out_v.at[g], out_ref.at[pl.ds(g * CHUNK, CHUNK)], sems.at[g])
        copy.start()
        copies.append(copy)
    for g in range(8):
        hg_out[:, pl.ds(g * CHUNK, CHUNK)] = hg_ref[g]
    loss_out[...] = loss_ref[0]
    for copy in copies:
        copy.wait()


def per_device(hidden_states, head_weight, teacher_codes, teacher_scales, targets):
    hidden = hidden_states.reshape(2, 8, CHUNK).transpose(1, 0, 2).reshape(2, 4, 2, CHUNK)
    scales = teacher_scales.reshape(2, 4, 128).transpose(1, 0, 2)
    codes = teacher_codes.reshape(2, 128, 512).transpose(1, 0, 2).reshape(2, 2, 4, 4, 2, 2, 512)
    weight = head_weight.reshape(8, CHUNK, 512)

    vmem = pltpu.VMEM
    scratch = [
        vmem((2, 4, 4, 4, 16, WIDE), BF16),
        vmem((8, CHUNK, 512), BF16),
        vmem((2, 4, 2, WIDE), BF16),
        vmem((2, 4, 2, WIDE), BF16),
        vmem((4, 2, 2, 4, 2, 2, 512), BF16),
        vmem((4, 4, 2, 4, 2, 512), BF16),
        vmem((4, 4, 4, 2, 2, 512), BF16),
        vmem((2, 4, 4, 4, 2, 512), BF16),
        vmem((256, 512), F32),
        vmem((256, 512), F32),
        vmem((8, 8, 256), F32),
        vmem((16, 8, 256), F32),
        vmem((4, 4, 4, 16, CHUNK), F32),
        vmem((4, 4, 4, 16, CHUNK), BF16),
        vmem((4, 4, 4, 16, CHUNK), BF16),
        vmem((4, 4, 4, 16, CHUNK), BF16),
    ]
    widths = [part[2] for part in PARTS]
    forwarded = [(4, 2, 16, widths[0]), (2, 2, 2, 16, widths[1]), (2, 2, 2, 16, widths[2])]
    arrived = [(4, 4, 16, widths[0]), (2, 2, 4, 16, widths[1]), (2, 2, 4, 16, widths[2])]
    scratch += [vmem(shape, BF16) for shape in forwarded * 2 + arrived * 2]
    scratch += [vmem((4, 4, 16, n), F32) for n in widths]
    scratch += [vmem((4, 4, 16, n), BF16) for n in widths]
    scratch += [vmem((3, 4, 16, n), BF16) for n in widths]
    scratch += [vmem((4, 16, n), F32) for n in widths]
    scratch += [vmem((3, 16, n), F32) for n in widths]
    scratch += [vmem((2, 4, 2, CHUNK), F32), vmem((2, 4, 2, CHUNK), F32)]
    scratch += [
        pltpu.SemaphoreType.DMA((176,)),
        pltpu.SemaphoreType.DMA((176,)),
        pltpu.SemaphoreType.DMA((16,)),
    ]
    hidden_grad, loss, grad, hidden_t = pl.pallas_call(
        kernel,
        out_shape=(
            pltpu.VMEM((2, 4, 2, CHUNK), F32),
            pltpu.VMEM((8, 256), F32),
            pltpu.VMEM((256, 512), BF16),
            pltpu.VMEM((8, CHUNK, 256), BF16),
        ),
        in_specs=[pl.BlockSpec(memory_space=pltpu.HBM)] * 4 + [pl.BlockSpec(memory_space=pltpu.VMEM)],
        out_specs=[pl.BlockSpec(memory_space=pltpu.VMEM)] * 4,
        scratch_shapes=scratch,
        compiler_params=pltpu.CompilerParams(
            collective_id=0, has_side_effects=True, vmem_limit_bytes=61500000
        ),
    )(hidden, weight, codes, scales, targets.reshape(1, 256))

    head_grad, hidden_grad, token_loss = pl.pallas_call(
        head_kernel,
        out_shape=(
            jax.ShapeDtypeStruct((8192, 512), BF16),
            jax.ShapeDtypeStruct((2, 8192), F32),
            jax.ShapeDtypeStruct((256,), F32),
        ),
        in_specs=[pl.BlockSpec(memory_space=pltpu.VMEM)] * 4,
        out_specs=[pl.BlockSpec(memory_space=pltpu.HBM)] + [pl.BlockSpec(memory_space=pltpu.VMEM)] * 2,
        scratch_shapes=[pltpu.VMEM((8, CHUNK, 512), BF16), pltpu.SemaphoreType.DMA((8,))],
        compiler_params=pltpu.CompilerParams(vmem_limit_bytes=40 * 1024 * 1024),
    )(hidden_t, grad, hidden_grad.reshape(8, 2, CHUNK), loss)
    return hidden_grad, head_grad, token_loss


def solution(mesh):
    return jax.shard_map(
        per_device,
        mesh=mesh,
        in_specs=(
            P(AXES, None),
            P(None, AXES),
            P(AXES, None),
            P(AXES, None),
            P(),
        ),
        out_specs=(P(AXES, None), P(None, AXES), P()),
        check_vma=False,
    )
```

```python
import functools

import jax
import jax.numpy as jnp
from jax import lax
from jax.experimental import pallas as pl
from jax.experimental.pallas import tpu as pltpu
from jax.sharding import PartitionSpec as P

GRAD_SCALE = 32.0
CE_WEIGHT = 0.5
F32, BF16 = jnp.float32, jnp.bfloat16
MESH = pl.DeviceIdType.MESH
AXES = ("dp", "vocab")

CHUNK = 1024
HALF = 4096
BLOCK_A, WIDE = 384, 1536
HIDDEN_C = HALF - 2 * WIDE
Z_ORDER = (2, 1, 3, 0)


def kernel(
    h_in, w_in, codes_in, scales_in, tgt_in,
    hg_out, loss_out, grad_out, ht_out,
    w_all, src, pre, send_a, recv_a, rows_b, rows_c, h_a, h_b, h_c,
    t1, t2, t3, t4, logits, teacher, st_a, st_b,
    own_a, own_b, own_c, to_a, to_b, to_c, from_a, from_b, from_c, sum_a, sum_b, sum_c,
    fl_a, fl_b, fl_c, fr_a, fr_b, fr_c, rl_a, rl_b, rl_c, rr_a, rr_b, rr_c,
    acc_a, acc_b, acc_c, out_a, out_b, out_c, in_a, in_b, in_c, keep_b,
    rest_a, rest_b, rest_c, last_a, last_b, last_c, fin_s, fin_r,
    send_sems, recv_sems, local_sems,
):
    dp, vo = lax.axis_index("dp"), lax.axis_index("vocab")
    me = {"x": vo // 8, "z": (vo // 2) % 4, "y": (dp // 2) * 2 + vo % 2, "c": dp % 2}

    def device(**other):
        at = {**me, **other}
        return ((at["y"] // 2) * 2 + at["c"], (at["x"] * 4 + at["z"]) * 2 + at["y"] % 2)

    def step(axis, k):
        return lax.rem(me[axis] + k, 2 if axis == "c" else 4)

    count = {"remote": 0, "local": 0}
    unsent = []

    def push(src, dst, **other):
        n = count["remote"]
        count["remote"] += 1
        copy = pltpu.make_async_remote_copy(
            src_ref=src, dst_ref=dst, send_sem=send_sems.at[n], recv_sem=recv_sems.at[n],
            device_id=device(**other), device_id_type=MESH,
        )
        copy.start()
        unsent.append(copy)
        return copy

    def local(src, dst):
        n = count["local"]
        count["local"] += 1
        copy = pltpu.make_async_copy(src, dst, local_sems.at[n])
        copy.start()
        return copy

    barrier = pltpu.get_barrier_semaphore()
    partners = [dict(x=step("x", i), y=step("y", k)) for i in range(4) for k in range(4) if (i, k) != (0, 0)]
    group = [(k, e) for k in range(4) for e in range(2) if (k, e) != (0, 0)]
    partners += [dict(z=step("z", k), c=step("c", e)) for k, e in group]
    for other in partners:
        pl.semaphore_signal(barrier, inc=1, device_id=device(**other), device_id_type=MESH)

    heads = [local(h_in.at[:, pl.ds(c * HALF, HALF)], src.at[c, :, pl.ds(0, HALF)]) for c in range(2)]
    heads += [local(scales_in, src.at[c, :, pl.ds(HALF, 512)]) for c in range(2)]
    own_codes = local(codes_in.at[:, :, me["x"]], t1.at[me["x"]])
    w_copy = local(w_in, w_all)
    k_row = lax.broadcasted_iota(jnp.int32, (256, 256), 0)
    n_col = lax.broadcasted_iota(jnp.int32, (256, 256), 1)
    natural = (
        ((k_row >> 5) & 1) * 128 + ((k_row >> 1) & 1) * 64 + (k_row >> 6) * 16
        + ((k_row >> 2) & 3) * 4 + ((k_row >> 4) & 1) * 2 + (k_row & 1)
    )
    reorder = natural == n_col
    target = jnp.sum(jnp.where(reorder, tgt_in[...].astype(F32), 0.0), axis=1, keepdims=True)
    first = (dp * 32 + vo) * 512
    hit = (first + lax.broadcasted_iota(jnp.int32, (256, 512), 1)).astype(F32) == target
    for copy in heads:
        copy.wait()
    pl.semaphore_wait(barrier, len(partners))

    other_core = step("c", 1)
    swap = push(src.at[other_core], pre.at[me["c"]], c=other_core)
    codes_wave = [push(codes_in.at[:, :, step("x", k)], t1.at[me["x"]], x=step("x", k)) for k in (2, 1, 3)]
    pre[me["c"]] = src[me["c"]]
    swap.wait_recv()
    rows = jnp.concatenate([pre[0].astype(F32), pre[1].astype(F32)], axis=0).astype(BF16)
    for z in range(4):
        send_a[z] = rows[:, z * BLOCK_A : (z + 1) * BLOCK_A]
    rows_b[me["y"], me["z"]] = rows[:, WIDE : 2 * WIDE]
    rows_c[me["x"], me["z"]] = rows[:, 2 * WIDE :]

    def spread(src_ref, dst_ref, axis):
        return [push(src_ref, dst_ref, **{axis: step(axis, k)}) for k in (2, 1, 3)]

    def pack(pieces):
        return jnp.concatenate([p.astype(F32) for p in pieces], axis=0).astype(BF16)

    wave_b = spread(rows_b.at[me["y"], me["z"]], rows_b.at[me["y"], me["z"]], "y")
    wave_c = spread(rows_c.at[me["x"], me["z"]], rows_c.at[me["x"], me["z"]], "z")
    wave_a = [push(send_a.at[step("z", k)], recv_a.at[me["z"]], z=step("z", k)) for k in (2, 1, 3)]
    recv_a[me["z"]] = send_a[me["z"]]
    own_codes.wait()

    for copy in wave_b:
        copy.wait_recv()
    wave_b = spread(rows_b.at[:, me["z"]], rows_b.at[:, me["z"]], "z")
    for copy in wave_c:
        copy.wait_recv()
    h_c[me["c"], me["x"], me["y"]] = pack([rows_c[me["x"], z] for z in range(4)])
    view = h_c.at[me["c"], me["x"], me["y"]]
    wave_c = spread(view, view, "x")
    for copy in wave_a:
        copy.wait_recv()
    h_a[me["c"], me["z"], me["x"], me["y"]] = pack([recv_a[z] for z in range(4)])
    view = h_a.at[me["c"], me["z"], me["x"], me["y"]]
    plane = [(i, k) for i in range(4) for k in range(4) if (i, k) != (0, 0)]
    wave_a = [push(view, view, x=step("x", i), y=step("y", k)) for i, k in plane]
    for copy in codes_wave:
        copy.wait_recv()
    codes_wave = [
        push(t1.at[:, step("y", k) // 2, :, :, step("y", k) % 2], t2.at[me["y"]], y=step("y", k))
        for k in (2, 1, 3)
    ]
    t2[me["y"]] = t1[:, me["y"] // 2, :, :, me["y"] % 2]

    full, half0, half1 = slice(None), pl.ds(0, 2), pl.ds(2, 2)
    ring_axis = ("z", "x", "y")

    def block(i, coordinate, half):
        if i == 0:
            return h_a.at[me["c"], coordinate, half]
        if i == 1:
            return h_b.at[me["c"], coordinate, half]
        return h_c.at[me["c"], half, coordinate]

    def ring(i, coordinate, half, k):
        view, axis = block(i, coordinate, half), ring_axis[i]
        return push(view, view, **{axis: step(axis, k)})

    crossing, right, left = [], [None] * 3, [None] * 3

    def cross(i, coordinate, half=full):
        view = block(i, coordinate, half)
        crossing.append(push(view, view, c=other_core))

    def start_ring(i):
        here = me[ring_axis[i]]
        up0, down1 = ring(i, here, half0, 1), ring(i, here, half1, 3)
        right[i] = [up0, ring(i, here, half1, 1)]
        left[i] = [ring(i, here, half0, 3), down1]

    for copy in wave_c:
        copy.wait_recv()
    start_ring(2)
    for copy in wave_b:
        copy.wait_recv()
    for y in range(4):
        h_b[me["c"], me["x"], y] = pack([rows_b[y, z] for z in range(4)])
    start_ring(1)
    for copy in wave_a:
        copy.wait_recv()
    start_ring(0)
    for i in (2, 1, 0):
        cross(i, me[ring_axis[i]])
    for copy in codes_wave:
        copy.wait_recv()
    codes_wave = [push(t2.at[:, :, :, step("z", k)], t3.at[me["z"]], z=step("z", k)) for k in (2, 1, 3)]
    t3[me["z"]] = t2[:, :, :, me["z"]]
    forward = [None] * 3
    for i in (2, 1, 0):
        right[i][0].wait_recv()
        up = ring(i, step(ring_axis[i], 3), half0, 1)
        left[i][1].wait_recv()
        forward[i] = (up, ring(i, step(ring_axis[i], 1), half1, 3))
    for i in (2, 1, 0):
        right[i][1].wait_recv()
        cross(i, step(ring_axis[i], 3))
        left[i][0].wait_recv()
        cross(i, step(ring_axis[i], 1))
    for copy in codes_wave:
        copy.wait_recv()
    codes_core = push(t3.at[:, :, :, other_core], t4.at[me["c"]], c=other_core)
    t4[me["c"]] = t3[:, :, :, me["c"]]
    for i in (2, 1, 0):
        forward[i][0].wait_recv()
        cross(i, step(ring_axis[i], 2), half0)
        forward[i][1].wait_recv()
        cross(i, step(ring_axis[i], 2), half1)

    w_copy.wait()
    logits[...] = jnp.zeros_like(logits)

    def add_logits(c):
        for ref, first, width in ((h_b, WIDE, WIDE), (h_c, 2 * WIDE, HIDDEN_C)):
            rows = ref[c, :, :, :, pl.ds(0, width)].reshape(256, width)
            logits[...] += jnp.dot(rows, w_all[c, pl.ds(first, width), :], preferred_element_type=F32)
        rows = jnp.concatenate([h_a[c, z].reshape(256, BLOCK_A) for z in range(4)], axis=1)
        logits[...] += jnp.dot(rows, w_all[c, pl.ds(0, WIDE), :], preferred_element_type=F32)

    add_logits(me["c"])
    block_row = lax.broadcasted_iota(jnp.int32, (512, 512), 0)
    column = lax.broadcasted_iota(jnp.int32, (512, 512), 1)
    pick = (block_row == dp * 128 + vo * 4 + column // 128).astype(F32).astype(BF16)
    scale = jnp.dot(
        h_c[me["c"], :, :, :, pl.ds(HIDDEN_C, 512)].reshape(256, 512), pick, preferred_element_type=F32
    )
    codes_core.wait_recv()
    for x in range(4):
        for y in range(4):
            row = (x * 4 + y) * 16
            code = jnp.concatenate(
                [t4[c, z, y, x].astype(F32) for z in range(4) for c in range(2)], axis=0
            )
            teacher[pl.ds(row, 16), :] = code * scale[row : row + 16]
    for copy in crossing:
        copy.wait_recv()
    add_logits(other_core)

    lg, tc = logits[...], teacher[...]
    m_s = jnp.max(lg, axis=1, keepdims=True)
    m_t = jnp.max(tc, axis=1, keepdims=True)
    w_t = jnp.exp(tc - m_t)
    stats = (
        m_s, jnp.sum(jnp.exp(lg - m_s), axis=1, keepdims=True),
        m_t, jnp.sum(w_t, axis=1, keepdims=True),
        jnp.sum(w_t * (tc - lg), axis=1, keepdims=True),
        jnp.sum(jnp.where(hit, lg, 0.0), axis=1, keepdims=True),
    )
    lane = lax.broadcasted_iota(jnp.int32, (256, 128), 1)
    packed = jnp.zeros((256, 128), F32)
    for n, value in enumerate(stats):
        packed = jnp.where(lane == n, value, packed)
    mine = packed.T[:8]

    def merge(parts):
        m1 = functools.reduce(jnp.maximum, [p[0:1] for p in parts])
        m2 = functools.reduce(jnp.maximum, [p[2:3] for p in parts])
        e1 = [jnp.exp(p[0:1] - m1) for p in parts]
        e2 = [jnp.exp(p[2:3] - m2) for p in parts]
        s1 = sum(p[1:2] * e for p, e in zip(parts, e1))
        s2 = sum(p[3:4] * e for p, e in zip(parts, e2))
        cross_sum = sum(p[4:5] * e for p, e in zip(parts, e2))
        target = sum(p[5:6] for p in parts)
        pad = jnp.zeros((2, 256), F32)
        return jnp.concatenate([m1, s1, m2, s2, cross_sum, target, pad], axis=0)

    def transpose_half(c):
        for z in range(4):
            ht_out[pl.ds(c * HALF + z * BLOCK_A, BLOCK_A), :] = h_a[c, z].reshape(256, BLOCK_A).T
        for ref, first, width in ((h_b, WIDE, WIDE), (h_c, 2 * WIDE, HIDDEN_C)):
            ht_out[pl.ds(c * HALF + first, width), :] = ref[c, :, :, :, pl.ds(0, width)].reshape(256, width).T

    st_a[0] = mine
    copies = [
        push(st_a.at[0], st_a.at[1 + n], z=step("z", k), c=step("c", e)) for n, (k, e) in enumerate(group)
    ]
    transpose_half(0)
    for copy in copies:
        copy.wait_recv()
    mine = merge([st_a[k] for k in range(8)])
    st_b[0] = mine
    copies = [
        push(st_b.at[0], st_b.at[1 + n], x=step("x", i), y=step("y", k)) for n, (i, k) in enumerate(plane)
    ]
    transpose_half(1)
    for copy in copies:
        copy.wait_recv()
    mine = merge([st_b[k] for k in range(16)])

    log_s = mine[0:1] + jnp.log(mine[1:2])
    log_t = mine[2:3] + jnp.log(mine[3:4])
    loss = mine[4:5] / mine[3:4] - log_t + log_s + CE_WEIGHT * (log_s - mine[5:6])
    columns = jnp.concatenate([log_s, log_t, loss, jnp.zeros((125, 256), F32)], axis=0).T
    grad = GRAD_SCALE * (
        (1.0 + CE_WEIGHT) * jnp.exp(logits[...] - columns[:, 0:1])
        - jnp.exp(teacher[...] - columns[:, 1:2])
        - CE_WEIGHT * hit.astype(F32)
    )
    grad_out[...] = grad.astype(BF16)

    own, to, came = (own_a, own_b, own_c), (to_a, to_b, to_c), (from_a, from_b, from_c)
    summed = (sum_a, sum_b, sum_c)
    fl, fr, rl, rr = (fl_a, fl_b, fl_c), (fr_a, fr_b, fr_c), (rl_a, rl_b, rl_c), (rr_a, rr_b, rr_c)
    widths = (BLOCK_A, WIDE // 2, HIDDEN_C // 2)
    first_of = (0, WIDE, 2 * WIDE)
    crossing, ring_waits = {}, {}

    def partial_of(c, i, n):
        if i == 0:
            first = pl.multiple_of(step("z", Z_ORDER[n]) * BLOCK_A, 128)
        else:
            first = first_of[i] + n * widths[i]
        return lax.dot_general(
            grad_out[...], w_all[c, pl.ds(first, widths[i]), :], (((1,), (1,)), ((), ())),
            preferred_element_type=F32,
        ).reshape(4, 4, 16, widths[i])

    def pieces(i, n):
        return (2 * n, 2 * n + 1) if i == 0 else (n,)

    def send_unit(i, n):
        for p in pieces(i, n):
            to[i][p] = partial_of(other_core, i, p).astype(BF16)
        index = pl.ds(2 * n, 2) if i == 0 else n
        crossing[i, n] = push(to[i].at[index], came[i].at[index], c=other_core)

    def own_unit(i, n):
        for p in pieces(i, n):
            own[i][p] = partial_of(me["c"], i, p)

    def add_unit(i, n):
        crossing[i, n].wait_recv()
        for p in pieces(i, n):
            total = own[i][p] + came[i][p].astype(F32)
            own[i][p] = total
            summed[i][p] = total.astype(BF16)

    def block_of(i, k, n, half):
        if i == 0:
            return (Z_ORDER.index(k), half)
        if i == 1:
            return (n, step("x", k), half)
        return (n, half, step("y", k))

    def ring_push(i, k, n, half, buffer, toward):
        axis = ring_axis[i]
        place = () if i == 0 else (n,)
        if buffer is rl or buffer is rr:
            place = (*place, half)
        target = buffer[i].at[place] if place else buffer[i]
        return push(summed[i].at[block_of(i, k, n, half)], target, **{axis: step(axis, toward)})

    def ring_opposite(i, n):
        ring_waits[i, n] = [ring_push(i, 2, n, half0, fl, 1), ring_push(i, 2, n, half1, fr, 3)]

    def ring_up(i, n):
        ring_waits[i, n].append(ring_push(i, 1, n, half1, rl, 1))

    def ring_down(i, n):
        ring_waits[i, n].append(ring_push(i, 3, n, half0, rr, 3))

    def ring_forward(i, n):
        waits = ring_waits[i, n]
        for m, (k, half, ref, buffer) in enumerate(((1, half0, fl, rl), (3, half1, fr, rr))):
            waits[m].wait_recv()
            index = block_of(i, k, n, half)
            carried = ref[i][...] if i == 0 else ref[i][n]
            summed[i][index] = (own[i][index] + carried.astype(F32)).astype(BF16)
            waits.append(ring_push(i, k, n, half, buffer, k))

    def start_unit(i, n):
        ring_opposite(i, n)
        ring_up(i, n)
        ring_down(i, n)

    send_unit(0, 0)
    send_unit(1, 0)
    own_unit(0, 0)
    add_unit(0, 0)
    ring_opposite(0, 0)
    ring_up(0, 0)
    send_unit(2, 0)
    own_unit(1, 0)
    add_unit(1, 0)
    start_unit(1, 0)
    send_unit(0, 1)
    own_unit(2, 0)
    add_unit(2, 0)
    start_unit(2, 0)
    send_unit(1, 1)
    own_unit(0, 1)
    add_unit(0, 1)
    ring_down(0, 0)
    send_unit(2, 1)
    own_unit(1, 1)
    add_unit(1, 1)
    start_unit(1, 1)
    ring_forward(0, 0)
    own_unit(2, 1)
    add_unit(2, 1)
    start_unit(2, 1)
    ring_forward(1, 0)
    ring_forward(2, 0)
    ring_forward(1, 1)
    ring_forward(2, 1)

    def ring_done(i):
        for n in range(1 if i == 0 else 2):
            for copy in ring_waits[i, n][2:]:
                copy.wait_recv()

    ring_done(0)
    acc_a[...] = own_a[3] + rl_a[...].astype(F32) + rr_a[...].astype(F32)
    out_a[...] = acc_a[...].astype(BF16)
    wave_a = [
        push(out_a.at[step("x", i), step("y", k)], in_a.at[n], x=step("x", i), y=step("y", k))
        for n, (i, k) in enumerate(plane)
    ]
    ring_done(1)
    for n in range(2):
        cols = pl.ds(n * widths[1], widths[1])
        acc_b[:, :, cols] = own_b[n, me["x"]] + rl_b[n].astype(F32) + rr_b[n].astype(F32)
    for z in range(4):
        piece = acc_b[:, pl.ds(z * 4, 4), :]
        keep_b[z] = piece
        out_b[z] = piece.astype(BF16)
    wave_b = [push(out_b.at[step("z", k)], in_b.at[k - 1], z=step("z", k)) for k in (2, 1, 3)]
    ring_done(2)
    for n in range(2):
        cols = pl.ds(n * widths[2], widths[2])
        acc_c[:, :, cols] = own_c[n, :, me["y"]] + rl_c[n].astype(F32) + rr_c[n].astype(F32)
    out_c[...] = acc_c[...].astype(BF16)
    wave_c = [push(out_c.at[step("x", k)], in_c.at[k - 1], x=step("x", k)) for k in (2, 1, 3)]
    loss_out[...] = jnp.broadcast_to(
        jnp.sum(jnp.where(reorder, columns[:, 2:3], 0.0), axis=0, keepdims=True), (8, 256)
    )

    for copy in wave_b:
        copy.wait_recv()
    total = keep_b[me["z"]]
    for n in range(3):
        total = total + in_b[n].astype(F32)
    rest_b[...] = total
    wave_b = [push(rest_b.at[step("y", k)], last_b.at[k - 1], y=step("y", k)) for k in (2, 1, 3)]
    for copy in wave_c:
        copy.wait_recv()
    total = acc_c[me["x"]]
    for n in range(3):
        total = total + in_c[n].astype(F32)
    for z in range(4):
        rest_c[z] = total[z * 4 : z * 4 + 4]
    wave_c = [push(rest_c.at[step("z", k)], last_c.at[k - 1], z=step("z", k)) for k in (2, 1, 3)]
    for copy in wave_a:
        copy.wait_recv()
    total = acc_a[me["x"], me["y"]]
    for n in range(15):
        total = total + in_a[n].astype(F32)
    for z in range(4):
        rest_a[z] = total[z * 4 : z * 4 + 4]
    wave_a = [push(rest_a.at[step("z", k)], last_a.at[me["z"]], z=step("z", k)) for k in (2, 1, 3)]
    last_a[me["z"]] = rest_a[me["z"]]

    def finish(total, first, width):
        for c in range(2):
            fin_s[c, :, pl.ds(first, width)] = total[c * 2 : c * 2 + 2]

    for copy in wave_b:
        copy.wait_recv()
    finish(rest_b[me["y"]] + last_b[0] + last_b[1] + last_b[2], WIDE, WIDE)
    for copy in wave_c:
        copy.wait_recv()
    finish(rest_c[me["z"]] + last_c[0] + last_c[1] + last_c[2], 2 * WIDE, HIDDEN_C)
    for copy in wave_a:
        copy.wait_recv()
    for z in range(4):
        finish(last_a[z], z * BLOCK_A, BLOCK_A)
    swap = push(fin_s.at[other_core], fin_r, c=other_core)
    hg_out[me["c"]] = fin_s[me["c"]]
    for copy in unsent[:-1]:
        copy.wait_send()
    swap.wait_recv()
    hg_out[other_core] = fin_r[...]
    swap.wait_send()


def head_kernel(ht_ref, grad_ref, hg_ref, loss_ref, out_ref, hg_out, loss_out, out_v, sems):
    copies = []
    for g in range(8):
        out_v[g] = jnp.dot(ht_ref[pl.ds(g * CHUNK, CHUNK), :], grad_ref[...], preferred_element_type=F32).astype(BF16)
        copy = pltpu.make_async_copy(out_v.at[g], out_ref.at[pl.ds(g * CHUNK, CHUNK)], sems.at[g])
        copy.start()
        copies.append(copy)
    for c in range(2):
        hg_out[:, pl.ds(c * HALF, HALF)] = hg_ref[c]
    loss_out[...] = loss_ref[0]
    for copy in copies:
        copy.wait()


def per_device(hidden_states, head_weight, teacher_codes, teacher_scales, targets):
    codes = teacher_codes.reshape(2, 128, 512).transpose(1, 0, 2).reshape(2, 2, 4, 4, 2, 2, 512)
    weight = head_weight.reshape(2, HALF, 512)

    vmem = pltpu.VMEM
    half_b, half_c = WIDE // 2, HIDDEN_C // 2
    unit_a, unit_b, unit_c = (4, 4, 4, 16, BLOCK_A), (2, 4, 4, 16, half_b), (2, 4, 4, 16, half_c)
    forwarded = ((2, 4, 16, BLOCK_A), (2, 2, 16, half_b), (2, 2, 16, half_c))
    arrived = ((4, 4, 16, BLOCK_A), (2, 4, 16, half_b), (2, 4, 16, half_c))
    scratch = [
        vmem((2, HALF, 512), BF16),
        vmem((2, 2, HALF + 512), BF16),
        vmem((2, 2, HALF + 512), BF16),
        vmem((4, 4, BLOCK_A), BF16),
        vmem((4, 4, BLOCK_A), BF16),
        vmem((4, 4, 4, WIDE), BF16),
        vmem((4, 4, 4, WIDE), BF16),
        vmem((2, 4, 4, 4, 16, BLOCK_A), BF16),
        vmem((2, 4, 4, 16, WIDE), BF16),
        vmem((2, 4, 4, 16, WIDE), BF16),
        vmem((4, 2, 2, 4, 2, 2, 512), BF16),
        vmem((4, 4, 2, 4, 2, 512), BF16),
        vmem((4, 4, 4, 2, 2, 512), BF16),
        vmem((2, 4, 4, 4, 2, 512), BF16),
        vmem((256, 512), F32),
        vmem((256, 512), F32),
        vmem((8, 8, 256), F32),
        vmem((16, 8, 256), F32),
    ]
    scratch += [vmem(shape, F32) for shape in (unit_a, unit_b, unit_c)]
    scratch += [vmem(shape, BF16) for shape in (unit_a, unit_b, unit_c) * 3]
    scratch += [vmem(shape, BF16) for shape in forwarded * 2 + arrived * 2]
    scratch += [
        vmem((4, 4, 16, BLOCK_A), F32),
        vmem((4, 16, WIDE), F32),
        vmem((4, 16, HIDDEN_C), F32),
        vmem((4, 4, 16, BLOCK_A), BF16),
        vmem((4, 4, 4, WIDE), BF16),
        vmem((4, 16, HIDDEN_C), BF16),
        vmem((15, 16, BLOCK_A), BF16),
        vmem((3, 4, 4, WIDE), BF16),
        vmem((3, 16, HIDDEN_C), BF16),
        vmem((4, 4, 4, WIDE), F32),
        vmem((4, 4, BLOCK_A), F32),
        vmem((4, 4, WIDE), F32),
        vmem((4, 4, HIDDEN_C), F32),
        vmem((4, 4, BLOCK_A), F32),
        vmem((3, 4, WIDE), F32),
        vmem((3, 4, HIDDEN_C), F32),
        vmem((2, 2, HALF), F32),
        vmem((2, HALF), F32),
        pltpu.SemaphoreType.DMA((208,)),
        pltpu.SemaphoreType.DMA((208,)),
        pltpu.SemaphoreType.DMA((8,)),
    ]
    hidden_grad, loss, grad, hidden_t = pl.pallas_call(
        kernel,
        out_shape=(
            pltpu.VMEM((2, 2, HALF), F32),
            pltpu.VMEM((8, 256), F32),
            pltpu.VMEM((256, 512), BF16),
            pltpu.VMEM((8192, 256), BF16),
        ),
        in_specs=[pl.BlockSpec(memory_space=pltpu.HBM)] * 4 + [pl.BlockSpec(memory_space=pltpu.VMEM)],
        out_specs=[pl.BlockSpec(memory_space=pltpu.VMEM)] * 4,
        scratch_shapes=scratch,
        compiler_params=pltpu.CompilerParams(
            collective_id=0, has_side_effects=True, vmem_limit_bytes=61500000
        ),
    )(hidden_states, weight, codes, teacher_scales, targets.reshape(1, 256))

    head_grad, hidden_grad, token_loss = pl.pallas_call(
        head_kernel,
        out_shape=(
            jax.ShapeDtypeStruct((8192, 512), BF16),
            jax.ShapeDtypeStruct((2, 8192), F32),
            jax.ShapeDtypeStruct((256,), F32),
        ),
        in_specs=[pl.BlockSpec(memory_space=pltpu.VMEM)] * 4,
        out_specs=[pl.BlockSpec(memory_space=pltpu.HBM)] + [pl.BlockSpec(memory_space=pltpu.VMEM)] * 2,
        scratch_shapes=[pltpu.VMEM((8, CHUNK, 512), BF16), pltpu.SemaphoreType.DMA((8,))],
        compiler_params=pltpu.CompilerParams(vmem_limit_bytes=40 * 1024 * 1024),
    )(hidden_t, grad, hidden_grad, loss)
    return hidden_grad, head_grad, token_loss


def solution(mesh):
    return jax.shard_map(
        per_device,
        mesh=mesh,
        in_specs=(
            P(AXES, None),
            P(None, AXES),
            P(AXES, None),
            P(AXES, None),
            P(),
        ),
        out_specs=(P(AXES, None), P(None, AXES), P()),
        check_vma=False,
    )
```

```python
import functools

import jax
import jax.numpy as jnp
from jax import lax
from jax.experimental import pallas as pl
from jax.experimental.pallas import tpu as pltpu
from jax.sharding import PartitionSpec as P

GRAD_SCALE = 32.0
CE_WEIGHT = 0.5
F32, BF16 = jnp.float32, jnp.bfloat16
MESH = pl.DeviceIdType.MESH
AXES = ("dp", "vocab")

CHUNK = 1024
HALF = 4096
BLOCK_A, PART_A, WIDE, HIDDEN_C = 256, 1024, 1664, 1408
SUM_BLOCK, SUM_A, SUM_WIDE = 384, 1536, 1280
Z_ORDER = (2, 1, 3, 0)


def kernel(
    h_in, w_in, codes_in, scales_in, tgt_in,
    hg_out, loss_out, head_out,
    w_all, grad_v, ht, src, recv_a, rows_b, rows_c, h_a, h_b, h_c,
    t1, t2, t3, t4, logits, teacher, st_a, st_b,
    own_a, own_b, own_c, to_a, to_b, to_c, from_a, from_b, from_c, sum_a, sum_b, sum_c,
    fl_a, fl_b, fl_c, fr_a, fr_b, fr_c, rl_a, rl_b, rl_c, rr_a, rr_b, rr_c,
    acc_a, acc_b, acc_c, out_a, out_b, out_c, in_a, in_b, in_c, keep_b,
    rest_a, rest_b, rest_c, last_a, last_b, last_c,
    send_sems, recv_sems, local_sems,
):
    dp, vo = lax.axis_index("dp"), lax.axis_index("vocab")
    me = {"x": vo // 8, "z": (vo // 2) % 4, "y": (dp // 2) * 2 + vo % 2, "c": dp % 2}

    def device(**other):
        at = {**me, **other}
        return ((at["y"] // 2) * 2 + at["c"], (at["x"] * 4 + at["z"]) * 2 + at["y"] % 2)

    def step(axis, k):
        return lax.rem(me[axis] + k, 2 if axis == "c" else 4)

    count = {"remote": 0, "local": 0}
    unsent = []

    def push(src, dst, **other):
        n = count["remote"]
        count["remote"] += 1
        copy = pltpu.make_async_remote_copy(
            src_ref=src, dst_ref=dst, send_sem=send_sems.at[n], recv_sem=recv_sems.at[n],
            device_id=device(**other), device_id_type=MESH,
        )
        copy.start()
        unsent.append(copy)
        return copy

    def local(src, dst):
        n = count["local"]
        count["local"] += 1
        copy = pltpu.make_async_copy(src, dst, local_sems.at[n])
        copy.start()
        return copy

    barrier = pltpu.get_barrier_semaphore()
    partners = [{axis: step(axis, k)} for axis in "xyz" for k in (2, 1, 3)]
    partners += [{axis: step(axis, k), "c": step("c", 1)} for axis in "yz" for k in (2, 1, 3)] + [dict(c=step("c", 1))]
    group = [(k, e) for k in range(4) for e in range(2) if (k, e) != (0, 0)]
    for other in partners:
        pl.semaphore_signal(barrier, inc=1, device_id=device(**other), device_id_type=MESH)

    heads = [local(h_in.at[:, pl.ds(c * HALF, HALF)], src.at[c, :, pl.ds(0, HALF)]) for c in range(2)]
    heads += [local(scales_in.at[:, pl.ds(c * 256, 256)], src.at[c, :, pl.ds(HALF, 256)]) for c in range(2)]
    own_codes = local(codes_in.at[:, :, me["x"]], t1.at[me["x"]])
    w_copy = local(w_in, w_all)
    k_row = lax.broadcasted_iota(jnp.int32, (256, 256), 0)
    n_col = lax.broadcasted_iota(jnp.int32, (256, 256), 1)
    natural = (
        ((k_row >> 5) & 1) * 128 + ((k_row >> 1) & 1) * 64 + (k_row >> 6) * 16
        + ((k_row >> 2) & 3) * 4 + ((k_row >> 4) & 1) * 2 + (k_row & 1)
    )
    reorder = natural == n_col
    target = jnp.sum(jnp.where(reorder, tgt_in[...].astype(F32), 0.0), axis=1, keepdims=True)
    first = (dp * 32 + vo) * 512
    hit = (first + lax.broadcasted_iota(jnp.int32, (256, 512), 1)).astype(F32) == target
    for copy in heads:
        copy.wait()
    pl.semaphore_wait(barrier, len(partners))

    other_core = step("c", 1)

    def spread(src_ref, dst_ref, axis):
        return [push(src_ref, dst_ref, **{axis: step(axis, k)}) for k in (2, 1, 3)]

    wave_a, wave_b, wave_c = [], [], []
    cols_b, cols_c = pl.ds(PART_A, WIDE), pl.ds(PART_A + WIDE, WIDE)
    for k, e in group:
        y, z, c = step("y", k), step("z", k), step("c", e)
        wave_b.append(push(src.at[c, :, cols_b], rows_b.at[me["y"], me["z"], me["c"]], y=y, c=c))
        wave_c.append(push(src.at[c, :, cols_c], rows_c.at[me["x"], me["z"], me["c"]], z=z, c=c))
        cols_a = pl.ds(pl.multiple_of(z * BLOCK_A, BLOCK_A), BLOCK_A)
        wave_a.append(push(src.at[c, :, cols_a], recv_a.at[me["z"], me["c"]], z=z, c=c))
    codes_wave = [push(codes_in.at[:, :, step("x", k)], t1.at[me["x"]], x=step("x", k)) for k in (2, 1, 3)]
    rows_b[me["y"], me["z"], me["c"]] = src[me["c"], :, cols_b]
    rows_c[me["x"], me["z"], me["c"]] = src[me["c"], :, cols_c]
    recv_a[me["z"], me["c"]] = src[me["c"], :, pl.ds(pl.multiple_of(me["z"] * BLOCK_A, BLOCK_A), BLOCK_A)]

    def pack(pieces):
        return jnp.concatenate([p.astype(F32) for p in pieces], axis=0).astype(BF16)

    own_codes.wait()

    for copy in wave_b:
        copy.wait_recv()
    wave_b = spread(rows_b.at[:, me["z"]], rows_b.at[:, me["z"]], "z")
    for copy in wave_c:
        copy.wait_recv()
    h_c[me["c"], me["x"], me["y"]] = pack([rows_c[me["x"], z, c] for z in range(4) for c in range(2)])
    view = h_c.at[me["c"], me["x"], me["y"]]
    wave_c = spread(view, view, "x")
    for copy in wave_a:
        copy.wait_recv()
    h_a[me["c"], me["z"], me["x"], me["y"]] = pack([recv_a[z, c] for z in range(4) for c in range(2)])
    view = h_a.at[me["c"], me["z"], me["x"], me["y"]]
    plane = [(i, k) for i in range(4) for k in range(4) if (i, k) != (0, 0)]
    wave_a = [push(view, view, x=step("x", i), y=step("y", k)) for i, k in plane]
    for copy in codes_wave:
        copy.wait_recv()
    codes_wave = [
        push(t1.at[:, step("y", k) // 2, :, :, step("y", k) % 2], t2.at[me["y"]], y=step("y", k))
        for k in (2, 1, 3)
    ]
    t2[me["y"]] = t1[:, me["y"] // 2, :, :, me["y"] % 2]

    full, half0, half1 = slice(None), pl.ds(0, 2), pl.ds(2, 2)
    ring_axis = ("z", "x", "y")

    def block(i, coordinate, half):
        if i == 0:
            return h_a.at[me["c"], coordinate, half]
        if i == 1:
            return h_b.at[me["c"], coordinate, half]
        return h_c.at[me["c"], half, coordinate]

    def ring(i, coordinate, half, k):
        view, axis = block(i, coordinate, half), ring_axis[i]
        return push(view, view, **{axis: step(axis, k)})

    crossing, right, left = [], [None] * 3, [None] * 3

    def cross(i, coordinate, half=full):
        view = block(i, coordinate, half)
        crossing.append(push(view, view, c=other_core))

    def start_ring(i):
        here = me[ring_axis[i]]
        right[i], left[i] = [], []
        for n in range(2):
            right[i].append(ring(i, here, n, 1))
            left[i].append(ring(i, here, 3 - n, 3))
        right[i].append(ring(i, here, half1, 1))
        left[i].append(ring(i, here, half0, 3))

    for copy in wave_c:
        copy.wait_recv()
    start_ring(2)
    for copy in wave_b:
        copy.wait_recv()
    for y in range(4):
        h_b[me["c"], me["x"], y] = pack([rows_b[y, z, c] for z in range(4) for c in range(2)])
    start_ring(1)
    for copy in wave_a:
        copy.wait_recv()
    start_ring(0)
    for i in (2, 1, 0):
        cross(i, me[ring_axis[i]])
    for copy in codes_wave:
        copy.wait_recv()
    codes_wave = [push(t2.at[:, :, :, step("z", k)], t3.at[me["z"]], z=step("z", k)) for k in (2, 1, 3)]
    t3[me["z"]] = t2[:, :, :, me["z"]]
    forward = [[], [], []]
    for n in range(2):
        for i in (2, 1, 0):
            right[i][n].wait_recv()
            forward[i].append(ring(i, step(ring_axis[i], 3), n, 1))
            left[i][n].wait_recv()
            forward[i].append(ring(i, step(ring_axis[i], 1), 3 - n, 3))
    for i in (2, 1, 0):
        right[i][2].wait_recv()
        cross(i, step(ring_axis[i], 3))
        left[i][2].wait_recv()
        cross(i, step(ring_axis[i], 1))
    for copy in codes_wave:
        copy.wait_recv()
    codes_core = push(t3.at[:, :, :, other_core], t4.at[me["c"]], c=other_core)
    t4[me["c"]] = t3[:, :, :, me["c"]]
    codes_core.wait_recv()
    for x in range(4):
        for y in range(4):
            teacher[pl.ds((x * 4 + y) * 16, 16), :] = jnp.concatenate(
                [t4[c, z, y, x].astype(F32) for z in range(4) for c in range(2)], axis=0
            )
    for i in (2, 1, 0):
        for copy in forward[i]:
            copy.wait_recv()
        cross(i, step(ring_axis[i], 2))

    w_copy.wait()
    logits[...] = jnp.zeros_like(logits)

    def add_logits(c):
        for ref, first, width in ((h_b, PART_A, WIDE), (h_c, PART_A + WIDE, HIDDEN_C)):
            rows = ref[c, :, :, :, pl.ds(0, width)].reshape(256, width)
            logits[...] += jnp.dot(rows, w_all[c, pl.ds(first, width), :], preferred_element_type=F32)
        rows = jnp.concatenate([h_a[c, z].reshape(256, BLOCK_A) for z in range(4)], axis=1)
        logits[...] += jnp.dot(rows, w_all[c, pl.ds(0, PART_A), :], preferred_element_type=F32)

    add_logits(me["c"])
    for copy in crossing:
        copy.wait_recv()
    block_row = lax.broadcasted_iota(jnp.int32, (256, 512), 0)
    column = lax.broadcasted_iota(jnp.int32, (256, 512), 1)
    pick = (block_row == (dp % 2) * 128 + vo * 4 + column // 128).astype(F32).astype(BF16)
    scales = h_c[dp // 2, :, :, :, pl.ds(HIDDEN_C, 256)].reshape(256, 256)
    teacher[...] *= jnp.dot(scales, pick, preferred_element_type=F32)
    add_logits(other_core)

    lg, tc = logits[...], teacher[...]
    m_s = jnp.max(lg, axis=1, keepdims=True)
    m_t = jnp.max(tc, axis=1, keepdims=True)
    w_t = jnp.exp(tc - m_t)
    stats = (
        m_s, jnp.sum(jnp.exp(lg - m_s), axis=1, keepdims=True),
        m_t, jnp.sum(w_t, axis=1, keepdims=True),
        jnp.sum(w_t * (tc - lg), axis=1, keepdims=True),
        jnp.sum(jnp.where(hit, lg, 0.0), axis=1, keepdims=True),
    )
    lane = lax.broadcasted_iota(jnp.int32, (256, 128), 1)
    packed = jnp.zeros((256, 128), F32)
    for n, value in enumerate(stats):
        packed = jnp.where(lane == n, value, packed)
    mine = packed.T[:8]

    def merge(parts):
        m1 = functools.reduce(jnp.maximum, [p[0:1] for p in parts])
        m2 = functools.reduce(jnp.maximum, [p[2:3] for p in parts])
        e1 = [jnp.exp(p[0:1] - m1) for p in parts]
        e2 = [jnp.exp(p[2:3] - m2) for p in parts]
        s1 = sum(p[1:2] * e for p, e in zip(parts, e1))
        s2 = sum(p[3:4] * e for p, e in zip(parts, e2))
        cross_sum = sum(p[4:5] * e for p, e in zip(parts, e2))
        target = sum(p[5:6] for p in parts)
        pad = jnp.zeros((2, 256), F32)
        return jnp.concatenate([m1, s1, m2, s2, cross_sum, target, pad], axis=0)

    def transpose_half(c):
        for z in range(4):
            ht[pl.ds(c * HALF + z * BLOCK_A, BLOCK_A), :] = h_a[c, z].reshape(256, BLOCK_A).T
        for ref, first, width in ((h_b, PART_A, WIDE), (h_c, PART_A + WIDE, HIDDEN_C)):
            ht[pl.ds(c * HALF + first, width), :] = ref[c, :, :, :, pl.ds(0, width)].reshape(256, width).T

    st_a[0] = mine
    copies = [
        push(st_a.at[0], st_a.at[1 + n], z=step("z", k), c=step("c", e)) for n, (k, e) in enumerate(group)
    ]
    transpose_half(0)
    for copy in copies:
        copy.wait_recv()
    mine = merge([st_a[k] for k in range(8)])
    st_b[0] = mine
    copies = [
        push(st_b.at[0], st_b.at[1 + n], x=step("x", i), y=step("y", k)) for n, (i, k) in enumerate(plane)
    ]
    transpose_half(1)
    for copy in copies:
        copy.wait_recv()
    mine = merge([st_b[k] for k in range(16)])

    log_s = mine[0:1] + jnp.log(mine[1:2])
    log_t = mine[2:3] + jnp.log(mine[3:4])
    loss = mine[4:5] / mine[3:4] - log_t + log_s + CE_WEIGHT * (log_s - mine[5:6])
    columns = jnp.concatenate([log_s, log_t, loss, jnp.zeros((125, 256), F32)], axis=0).T
    grad = GRAD_SCALE * (
        (1.0 + CE_WEIGHT) * jnp.exp(logits[...] - columns[:, 0:1])
        - jnp.exp(teacher[...] - columns[:, 1:2])
        - CE_WEIGHT * hit.astype(F32)
    )
    grad_v[...] = grad.astype(BF16)

    own, to, came = (own_a, own_b, own_c), (to_a, to_b, to_c), (from_a, from_b, from_c)
    summed = (sum_a, sum_b, sum_c)
    fl, fr, rl, rr = (fl_a, fl_b, fl_c), (fr_a, fr_b, fr_c), (rl_a, rl_b, rl_c), (rr_a, rr_b, rr_c)
    widths = (SUM_BLOCK, SUM_WIDE // 2, SUM_WIDE // 2)
    first_of = (0, SUM_A, SUM_A + SUM_WIDE)
    crossing, ring_waits = {}, {}

    def partial_of(c, i, n):
        if i == 0:
            first = pl.multiple_of(step("z", Z_ORDER[n]) * SUM_BLOCK, 128)
        else:
            first = first_of[i] + n * widths[i]
        return lax.dot_general(
            grad_v[...], w_all[c, pl.ds(first, widths[i]), :], (((1,), (1,)), ((), ())),
            preferred_element_type=F32,
        ).reshape(4, 4, 16, widths[i])

    def pieces(i, n):
        return (2 * n, 2 * n + 1) if i == 0 else (n,)

    def send_unit(i, n):
        for p in pieces(i, n):
            to[i][p] = partial_of(other_core, i, p).astype(BF16)
        index = pl.ds(2 * n, 2) if i == 0 else n
        crossing[i, n] = push(to[i].at[index], came[i].at[index], c=other_core)

    def own_unit(i, n):
        for p in pieces(i, n):
            own[i][p] = partial_of(me["c"], i, p)

    def add_unit(i, n):
        crossing[i, n].wait_recv()
        for p in pieces(i, n):
            total = own[i][p] + came[i][p].astype(F32)
            own[i][p] = total
            summed[i][p] = total.astype(BF16)

    def block_of(i, k, n, half):
        if i == 0:
            return (Z_ORDER.index(k), half)
        if i == 1:
            return (n, step("x", k), half)
        return (n, half, step("y", k))

    def ring_push(i, k, n, half, buffer, toward):
        axis = ring_axis[i]
        place = () if i == 0 else (n,)
        if buffer is rl or buffer is rr:
            place = (*place, half)
        target = buffer[i].at[place] if place else buffer[i]
        return push(summed[i].at[block_of(i, k, n, half)], target, **{axis: step(axis, toward)})

    def ring_opposite(i, n):
        ring_waits[i, n] = [ring_push(i, 2, n, half0, fl, 1), ring_push(i, 2, n, half1, fr, 3)]

    def ring_up(i, n):
        ring_waits[i, n].append(ring_push(i, 1, n, half1, rl, 1))

    def ring_down(i, n):
        ring_waits[i, n].append(ring_push(i, 3, n, half0, rr, 3))

    def ring_forward(i, n):
        waits = ring_waits[i, n]
        for m, (k, half, ref, buffer) in enumerate(((1, half0, fl, rl), (3, half1, fr, rr))):
            waits[m].wait_recv()
            index = block_of(i, k, n, half)
            carried = ref[i][...] if i == 0 else ref[i][n]
            summed[i][index] = (own[i][index] + carried.astype(F32)).astype(BF16)
            waits.append(ring_push(i, k, n, half, buffer, k))

    def start_unit(i, n):
        ring_opposite(i, n)
        ring_up(i, n)
        ring_down(i, n)

    def head_chunks(first, last):
        for n in range(first, last):
            chunk = pl.ds(n * CHUNK, CHUNK)
            head_out[chunk, :] = jnp.dot(ht[chunk, :], grad_v[...], preferred_element_type=F32).astype(BF16)

    send_unit(0, 0)
    send_unit(1, 0)
    own_unit(0, 0)
    add_unit(0, 0)
    ring_opposite(0, 0)
    ring_up(0, 0)
    send_unit(2, 0)
    own_unit(1, 0)
    add_unit(1, 0)
    start_unit(1, 0)
    send_unit(1, 1)
    own_unit(2, 0)
    add_unit(2, 0)
    start_unit(2, 0)
    send_unit(2, 1)
    own_unit(1, 1)
    add_unit(1, 1)
    start_unit(1, 1)
    send_unit(0, 1)
    own_unit(2, 1)
    add_unit(2, 1)
    start_unit(2, 1)
    own_unit(0, 1)
    add_unit(0, 1)
    ring_down(0, 0)
    ring_forward(0, 0)
    head_chunks(0, 1)
    ring_forward(1, 0)
    ring_forward(2, 0)
    ring_forward(1, 1)
    ring_forward(2, 1)
    head_chunks(1, 3)

    def ring_done(i):
        for n in range(1 if i == 0 else 2):
            for copy in ring_waits[i, n][2:]:
                copy.wait_recv()

    ring_done(0)
    acc_a[...] = own_a[3] + rl_a[...].astype(F32) + rr_a[...].astype(F32)
    out_a[...] = acc_a[...].astype(BF16)
    wave_a = [
        push(out_a.at[step("x", i), step("y", k)], in_a.at[n], x=step("x", i), y=step("y", k))
        for n, (i, k) in enumerate(plane)
    ]
    ring_done(1)
    for n in range(2):
        cols = pl.ds(n * widths[1], widths[1])
        acc_b[:, :, cols] = own_b[n, me["x"]] + rl_b[n].astype(F32) + rr_b[n].astype(F32)
    for z in range(4):
        piece = acc_b[:, pl.ds(z * 4, 4), :]
        keep_b[z] = piece
        out_b[z] = piece.astype(BF16)
    wave_b = [push(out_b.at[step("z", k)], in_b.at[k - 1], z=step("z", k)) for k in (2, 1, 3)]
    ring_done(2)
    for n in range(2):
        cols = pl.ds(n * widths[2], widths[2])
        acc_c[:, :, cols] = own_c[n, :, me["y"]] + rl_c[n].astype(F32) + rr_c[n].astype(F32)
    out_c[...] = acc_c[...].astype(BF16)
    wave_c = [push(out_c.at[step("x", k)], in_c.at[k - 1], x=step("x", k)) for k in (2, 1, 3)]
    head_chunks(3, 6)
    loss_out[...] = jnp.broadcast_to(
        jnp.sum(jnp.where(reorder, columns[:, 2:3], 0.0), axis=0, keepdims=True), (8, 256)
    )

    for copy in wave_b:
        copy.wait_recv()
    total = keep_b[me["z"]]
    for n in range(3):
        total = total + in_b[n].astype(F32)
    for c in range(2):
        rest_b[:, c] = total[:, c * 2 : c * 2 + 2]

    def last_step(rest, last, axis):
        copies = [
            push(rest.at[step(axis, k), step("c", e)], last.at[e * 4 + k], **{axis: step(axis, k)}, c=step("c", e))
            for k, e in group
        ]
        last[0] = rest[me[axis], me["c"]]
        return copies

    wave_b = last_step(rest_b, last_b, "y")
    for copy in wave_c:
        copy.wait_recv()
    total = acc_c[me["x"]]
    for n in range(3):
        total = total + in_c[n].astype(F32)
    for z in range(4):
        for c in range(2):
            rest_c[z, c] = total[z * 4 + c * 2 : z * 4 + c * 2 + 2]
    wave_c = last_step(rest_c, last_c, "z")
    for copy in wave_a:
        copy.wait_recv()
    total = acc_a[me["x"], me["y"]]
    for n in range(15):
        total = total + in_a[n].astype(F32)
    for z in range(4):
        for c in range(2):
            rest_a[z, c] = total[z * 4 + c * 2 : z * 4 + c * 2 + 2]
    wave_a = []
    for k, e in group:
        z, c = step("z", k), step("c", e)
        wave_a.append(push(rest_a.at[z, c], last_a.at[me["z"], me["c"]], z=z, c=c))
    last_a[me["z"], me["c"]] = rest_a[me["z"], me["c"]]
    head_chunks(6, 8)

    for wave, last, first in ((wave_b, last_b, SUM_A), (wave_c, last_c, SUM_A + SUM_WIDE)):
        for copy in wave:
            copy.wait_recv()
        for e in range(2):
            total = last[e * 4] + last[e * 4 + 1] + last[e * 4 + 2] + last[e * 4 + 3]
            hg_out[step("c", e), :, pl.ds(first, SUM_WIDE)] = total
    for copy in wave_a:
        copy.wait_recv()
    for z in range(4):
        for c in range(2):
            hg_out[c, :, pl.ds(z * SUM_BLOCK, SUM_BLOCK)] = last_a[z, c]
    for copy in unsent:
        copy.wait_send()


def store_kernel(head_ref, hg_ref, loss_ref, head_out, hg_out, loss_out, sems):
    copies = []
    for n in range(8):
        chunk = pl.ds(n * CHUNK, CHUNK)
        copies.append(pltpu.make_async_copy(head_ref.at[chunk], head_out.at[chunk], sems.at[n]))
        copies[n].start()
    for c in range(2):
        hg_out[:, pl.ds(c * HALF, HALF)] = hg_ref[c]
    loss_out[...] = loss_ref[0]
    for copy in copies:
        copy.wait()


def per_device(hidden_states, head_weight, teacher_codes, teacher_scales, targets):
    codes = teacher_codes.reshape(2, 128, 512).transpose(1, 0, 2).reshape(2, 2, 4, 4, 2, 2, 512)
    weight = head_weight.reshape(2, HALF, 512)

    vmem = pltpu.VMEM
    unit_a, unit_b = (4, 4, 4, 16, SUM_BLOCK), (2, 4, 4, 16, SUM_WIDE // 2)
    forwarded_a, forwarded_b = (2, 4, 16, SUM_BLOCK), (2, 2, 16, SUM_WIDE // 2)
    arrived_a, arrived_b = (4, 4, 16, SUM_BLOCK), (2, 4, 16, SUM_WIDE // 2)
    units = (unit_a, unit_b, unit_b)
    forwarded, arrived = (forwarded_a, forwarded_b, forwarded_b), (arrived_a, arrived_b, arrived_b)
    scratch = [
        vmem((2, HALF, 512), BF16),
        vmem((256, 512), BF16),
        vmem((8192, 256), BF16),
        vmem((2, 2, HALF + 256), BF16),
        vmem((4, 2, 2, BLOCK_A), BF16),
        vmem((4, 4, 2, 2, WIDE), BF16),
        vmem((4, 4, 2, 2, WIDE), BF16),
        vmem((2, 4, 4, 4, 16, BLOCK_A), BF16),
        vmem((2, 4, 4, 16, WIDE), BF16),
        vmem((2, 4, 4, 16, WIDE), BF16),
        vmem((4, 2, 2, 4, 2, 2, 512), BF16),
        vmem((4, 4, 2, 4, 2, 512), BF16),
        vmem((4, 4, 4, 2, 2, 512), BF16),
        vmem((2, 4, 4, 4, 2, 512), BF16),
        vmem((256, 512), F32),
        vmem((256, 512), F32),
        vmem((8, 8, 256), F32),
        vmem((16, 8, 256), F32),
    ]
    scratch += [vmem(shape, F32) for shape in units]
    scratch += [vmem(shape, BF16) for shape in units * 3]
    scratch += [vmem(shape, BF16) for shape in forwarded * 2 + arrived * 2]
    scratch += [
        vmem((4, 4, 16, SUM_BLOCK), F32),
        vmem((4, 16, SUM_WIDE), F32),
        vmem((4, 16, SUM_WIDE), F32),
        vmem((4, 4, 16, SUM_BLOCK), BF16),
        vmem((4, 4, 4, SUM_WIDE), BF16),
        vmem((4, 16, SUM_WIDE), BF16),
        vmem((15, 16, SUM_BLOCK), BF16),
        vmem((3, 4, 4, SUM_WIDE), BF16),
        vmem((3, 16, SUM_WIDE), BF16),
        vmem((4, 4, 4, SUM_WIDE), F32),
        vmem((4, 2, 2, SUM_BLOCK), F32),
        vmem((4, 2, 2, SUM_WIDE), F32),
        vmem((4, 2, 2, SUM_WIDE), F32),
        vmem((4, 2, 2, SUM_BLOCK), F32),
        vmem((8, 2, SUM_WIDE), F32),
        vmem((8, 2, SUM_WIDE), F32),
        pltpu.SemaphoreType.DMA((248,)),
        pltpu.SemaphoreType.DMA((248,)),
        pltpu.SemaphoreType.DMA((8,)),
    ]
    hidden_grad, loss, head_grad = pl.pallas_call(
        kernel,
        out_shape=(
            pltpu.VMEM((2, 2, HALF), F32),
            pltpu.VMEM((8, 256), F32),
            pltpu.VMEM((8192, 512), BF16),
        ),
        in_specs=[pl.BlockSpec(memory_space=pltpu.HBM)] * 4 + [pl.BlockSpec(memory_space=pltpu.VMEM)],
        out_specs=[pl.BlockSpec(memory_space=pltpu.VMEM)] * 3,
        scratch_shapes=scratch,
        compiler_params=pltpu.CompilerParams(
            collective_id=0, has_side_effects=True, vmem_limit_bytes=57500000
        ),
    )(hidden_states, weight, codes, teacher_scales, targets.reshape(1, 256))

    head_grad, hidden_grad, token_loss = pl.pallas_call(
        store_kernel,
        out_shape=(
            jax.ShapeDtypeStruct((8192, 512), BF16),
            jax.ShapeDtypeStruct((2, 8192), F32),
            jax.ShapeDtypeStruct((256,), F32),
        ),
        in_specs=[pl.BlockSpec(memory_space=pltpu.VMEM)] * 3,
        out_specs=[pl.BlockSpec(memory_space=pltpu.HBM)] + [pl.BlockSpec(memory_space=pltpu.VMEM)] * 2,
        scratch_shapes=[pltpu.SemaphoreType.DMA((8,))],
        compiler_params=pltpu.CompilerParams(vmem_limit_bytes=40 * 1024 * 1024),
    )(head_grad, hidden_grad, loss)
    return hidden_grad, head_grad, token_loss


def solution(mesh):
    return jax.shard_map(
        per_device,
        mesh=mesh,
        in_specs=(
            P(AXES, None),
            P(None, AXES),
            P(AXES, None),
            P(AXES, None),
            P(),
        ),
        out_specs=(P(AXES, None), P(None, AXES), P()),
        check_vma=False,
    )
```

```python
import functools

import jax
import jax.numpy as jnp
from jax import lax
from jax.experimental import pallas as pl
from jax.experimental.pallas import tpu as pltpu
from jax.sharding import PartitionSpec as P

GRAD_SCALE = 32.0
CE_WEIGHT = 0.5
F32, BF16 = jnp.float32, jnp.bfloat16
MESH = pl.DeviceIdType.MESH
AXES = ("dp", "vocab")

CHUNK = 1024
HALF = 4096
BLOCK_A, PART_A, WIDE, HIDDEN_C = 256, 1024, 1664, 1408
SUM_BLOCK, SUM_A, SUM_WIDE = 384, 1536, 1280
Z_ORDER = (2, 1, 3, 0)


def kernel(
    h_in, w_in, codes_in, scales_in, tgt_in,
    hg_out, loss_out, head_out,
    w_all, grad_v, ht, src, recv_a, rows_b, rows_c, h_a, h_b, h_c,
    t1, t2, t3, t4, logits, teacher, st_a, st_b,
    own_a, own_b, own_c, to_a, to_b, to_c, from_a, from_b, from_c, sum_a, sum_b, sum_c,
    fl_a, fl_b, fl_c, fr_a, fr_b, fr_c, rl_a, rl_b, rl_c, rr_a, rr_b, rr_c, ro_b, ro_c,
    acc_a, acc_b, acc_c, out_a, out_b, out_c, in_a, in_b, in_c, keep_b,
    rest_a, rest_b, rest_c, last_a, last_b, last_c,
    send_sems, recv_sems, local_sems,
):
    dp, vo = lax.axis_index("dp"), lax.axis_index("vocab")
    me = {"x": vo // 8, "z": (vo // 2) % 4, "y": (dp // 2) * 2 + vo % 2, "c": dp % 2}

    def device(**other):
        at = {**me, **other}
        return ((at["y"] // 2) * 2 + at["c"], (at["x"] * 4 + at["z"]) * 2 + at["y"] % 2)

    def step(axis, k):
        return lax.rem(me[axis] + k, 2 if axis == "c" else 4)

    count = {"remote": 0, "local": 0}
    unsent = []

    def push(src, dst, **other):
        n = count["remote"]
        count["remote"] += 1
        copy = pltpu.make_async_remote_copy(
            src_ref=src, dst_ref=dst, send_sem=send_sems.at[n], recv_sem=recv_sems.at[n],
            device_id=device(**other), device_id_type=MESH,
        )
        copy.start()
        unsent.append(copy)
        return copy

    def local(src, dst):
        n = count["local"]
        count["local"] += 1
        copy = pltpu.make_async_copy(src, dst, local_sems.at[n])
        copy.start()
        return copy

    barrier = pltpu.get_barrier_semaphore()
    partners = [{axis: step(axis, k)} for axis in "xyz" for k in (2, 1, 3)]
    partners += [{axis: step(axis, k), "c": step("c", 1)} for axis in "yz" for k in (2, 1, 3)] + [dict(c=step("c", 1))]
    group = [(k, e) for k in range(4) for e in range(2) if (k, e) != (0, 0)]
    for other in partners:
        pl.semaphore_signal(barrier, inc=1, device_id=device(**other), device_id_type=MESH)

    heads = [local(h_in.at[:, pl.ds(c * HALF, HALF)], src.at[c, :, pl.ds(0, HALF)]) for c in range(2)]
    heads += [local(scales_in.at[:, pl.ds(c * 256, 256)], src.at[c, :, pl.ds(HALF, 256)]) for c in range(2)]
    own_codes = local(codes_in.at[:, :, me["x"]], t1.at[me["x"]])
    w_copy = local(w_in, w_all)
    k_row = lax.broadcasted_iota(jnp.int32, (256, 256), 0)
    n_col = lax.broadcasted_iota(jnp.int32, (256, 256), 1)
    natural = (
        ((k_row >> 5) & 1) * 128 + ((k_row >> 1) & 1) * 64 + (k_row >> 6) * 16
        + ((k_row >> 2) & 3) * 4 + ((k_row >> 4) & 1) * 2 + (k_row & 1)
    )
    reorder = natural == n_col
    target = jnp.sum(jnp.where(reorder, tgt_in[...].astype(F32), 0.0), axis=1, keepdims=True)
    first = (dp * 32 + vo) * 512
    hit = (first + lax.broadcasted_iota(jnp.int32, (256, 512), 1)).astype(F32) == target
    for copy in heads:
        copy.wait()
    pl.semaphore_wait(barrier, len(partners))

    other_core = step("c", 1)

    def spread(src_ref, dst_ref, axis):
        return [push(src_ref, dst_ref, **{axis: step(axis, k)}) for k in (2, 1, 3)]

    wave_a, wave_b, wave_c = [], [], []
    cols_b, cols_c = pl.ds(PART_A, WIDE), pl.ds(PART_A + WIDE, WIDE)
    for k, e in group:
        y, z, c = step("y", k), step("z", k), step("c", e)
        wave_b.append(push(src.at[c, :, cols_b], rows_b.at[me["y"], me["z"], me["c"]], y=y, c=c))
        wave_c.append(push(src.at[c, :, cols_c], rows_c.at[me["x"], me["z"], me["c"]], z=z, c=c))
        cols_a = pl.ds(pl.multiple_of(z * BLOCK_A, BLOCK_A), BLOCK_A)
        wave_a.append(push(src.at[c, :, cols_a], recv_a.at[me["z"], me["c"]], z=z, c=c))
    codes_wave = [push(codes_in.at[:, :, step("x", k)], t1.at[me["x"]], x=step("x", k)) for k in (2, 1, 3)]
    rows_b[me["y"], me["z"], me["c"]] = src[me["c"], :, cols_b]
    rows_c[me["x"], me["z"], me["c"]] = src[me["c"], :, cols_c]
    recv_a[me["z"], me["c"]] = src[me["c"], :, pl.ds(pl.multiple_of(me["z"] * BLOCK_A, BLOCK_A), BLOCK_A)]

    def pack(pieces):
        return jnp.concatenate([p.astype(F32) for p in pieces], axis=0).astype(BF16)

    own_codes.wait()

    for copy in wave_b:
        copy.wait_recv()
    wave_b = spread(rows_b.at[:, me["z"]], rows_b.at[:, me["z"]], "z")
    for copy in wave_c:
        copy.wait_recv()
    h_c[me["c"], me["x"], me["y"]] = pack([rows_c[me["x"], z, c] for z in range(4) for c in range(2)])
    view = h_c.at[me["c"], me["x"], me["y"]]
    wave_c = spread(view, view, "x")
    for copy in wave_a:
        copy.wait_recv()
    h_a[me["c"], me["z"], me["x"], me["y"]] = pack([recv_a[z, c] for z in range(4) for c in range(2)])
    view = h_a.at[me["c"], me["z"], me["x"], me["y"]]
    plane = [(i, k) for i in range(4) for k in range(4) if (i, k) != (0, 0)]
    wave_a = [push(view, view, x=step("x", i), y=step("y", k)) for i, k in plane]
    for copy in codes_wave:
        copy.wait_recv()
    codes_wave = [
        push(t1.at[:, step("y", k) // 2, :, :, step("y", k) % 2], t2.at[me["y"]], y=step("y", k))
        for k in (2, 1, 3)
    ]
    t2[me["y"]] = t1[:, me["y"] // 2, :, :, me["y"] % 2]

    full, half0, half1 = slice(None), pl.ds(0, 2), pl.ds(2, 2)
    ring_axis = ("z", "x", "y")

    def block(i, coordinate, half):
        if i == 0:
            return h_a.at[me["c"], coordinate, half]
        if i == 1:
            return h_b.at[me["c"], coordinate, half]
        return h_c.at[me["c"], half, coordinate]

    def ring(i, coordinate, half, k):
        view, axis = block(i, coordinate, half), ring_axis[i]
        return push(view, view, **{axis: step(axis, k)})

    crossing, right, left = [], [None] * 3, [None] * 3

    def cross(i, coordinate, half=full):
        view = block(i, coordinate, half)
        crossing.append(push(view, view, c=other_core))

    def start_ring(i):
        here = me[ring_axis[i]]
        right[i], left[i] = [], []
        for n in range(2):
            right[i].append(ring(i, here, n, 1))
            left[i].append(ring(i, here, 3 - n, 3))
        right[i].append(ring(i, here, half1, 1))
        left[i].append(ring(i, here, half0, 3))

    for copy in wave_c:
        copy.wait_recv()
    start_ring(2)
    for copy in codes_wave:
        copy.wait_recv()
    codes_wave = [push(t2.at[:, :, :, step("z", k)], t3.at[me["z"]], z=step("z", k)) for k in (2, 1, 3)]
    t3[me["z"]] = t2[:, :, :, me["z"]]
    for copy in wave_b:
        copy.wait_recv()
    for y in range(4):
        h_b[me["c"], me["x"], y] = pack([rows_b[y, z, c] for z in range(4) for c in range(2)])
    start_ring(1)
    for copy in wave_a:
        copy.wait_recv()
    start_ring(0)
    for i in (2, 1, 0):
        cross(i, me[ring_axis[i]])
    forward = [[], [], []]
    for n in range(2):
        for i in (2, 1, 0):
            right[i][n].wait_recv()
            forward[i].append(ring(i, step(ring_axis[i], 3), n, 1))
            left[i][n].wait_recv()
            forward[i].append(ring(i, step(ring_axis[i], 1), 3 - n, 3))
    for i in (2, 1, 0):
        right[i][2].wait_recv()
        cross(i, step(ring_axis[i], 3))
        left[i][2].wait_recv()
        cross(i, step(ring_axis[i], 1))
    for copy in codes_wave:
        copy.wait_recv()
    codes_core = push(t3.at[:, :, :, other_core], t4.at[me["c"]], c=other_core)
    t4[me["c"]] = t3[:, :, :, me["c"]]
    codes_core.wait_recv()
    for x in range(4):
        for y in range(4):
            teacher[pl.ds((x * 4 + y) * 16, 16), :] = jnp.concatenate(
                [t4[c, z, y, x].astype(F32) for z in range(4) for c in range(2)], axis=0
            )
    for i in (2, 1, 0):
        for copy in forward[i]:
            copy.wait_recv()
        cross(i, step(ring_axis[i], 2))

    w_copy.wait()
    logits[...] = jnp.zeros_like(logits)

    def add_logits(c):
        for ref, first, width in ((h_b, PART_A, WIDE), (h_c, PART_A + WIDE, HIDDEN_C)):
            rows = ref[c, :, :, :, pl.ds(0, width)].reshape(256, width)
            logits[...] += jnp.dot(rows, w_all[c, pl.ds(first, width), :], preferred_element_type=F32)
        rows = jnp.concatenate([h_a[c, z].reshape(256, BLOCK_A) for z in range(4)], axis=1)
        logits[...] += jnp.dot(rows, w_all[c, pl.ds(0, PART_A), :], preferred_element_type=F32)

    add_logits(me["c"])
    for copy in crossing:
        copy.wait_recv()
    block_row = lax.broadcasted_iota(jnp.int32, (256, 512), 0)
    column = lax.broadcasted_iota(jnp.int32, (256, 512), 1)
    pick = (block_row == (dp % 2) * 128 + vo * 4 + column // 128).astype(F32).astype(BF16)
    scales = h_c[dp // 2, :, :, :, pl.ds(HIDDEN_C, 256)].reshape(256, 256)
    teacher[...] *= jnp.dot(scales, pick, preferred_element_type=F32)
    add_logits(other_core)

    lg, tc = logits[...], teacher[...]
    m_s = jnp.max(lg, axis=1, keepdims=True)
    m_t = jnp.max(tc, axis=1, keepdims=True)
    w_t = jnp.exp(tc - m_t)
    stats = (
        m_s, jnp.sum(jnp.exp(lg - m_s), axis=1, keepdims=True),
        m_t, jnp.sum(w_t, axis=1, keepdims=True),
        jnp.sum(w_t * (tc - lg), axis=1, keepdims=True),
        jnp.sum(jnp.where(hit, lg, 0.0), axis=1, keepdims=True),
    )
    lane = lax.broadcasted_iota(jnp.int32, (256, 128), 1)
    packed = jnp.zeros((256, 128), F32)
    for n, value in enumerate(stats):
        packed = jnp.where(lane == n, value, packed)
    mine = packed.T[:8]

    def merge(parts):
        m1 = functools.reduce(jnp.maximum, [p[0:1] for p in parts])
        m2 = functools.reduce(jnp.maximum, [p[2:3] for p in parts])
        e1 = [jnp.exp(p[0:1] - m1) for p in parts]
        e2 = [jnp.exp(p[2:3] - m2) for p in parts]
        s1 = sum(p[1:2] * e for p, e in zip(parts, e1))
        s2 = sum(p[3:4] * e for p, e in zip(parts, e2))
        cross_sum = sum(p[4:5] * e for p, e in zip(parts, e2))
        target = sum(p[5:6] for p in parts)
        pad = jnp.zeros((2, 256), F32)
        return jnp.concatenate([m1, s1, m2, s2, cross_sum, target, pad], axis=0)

    def transpose_half(c):
        for z in range(4):
            ht[pl.ds(c * HALF + z * BLOCK_A, BLOCK_A), :] = h_a[c, z].reshape(256, BLOCK_A).T
        for ref, first, width in ((h_b, PART_A, WIDE), (h_c, PART_A + WIDE, HIDDEN_C)):
            ht[pl.ds(c * HALF + first, width), :] = ref[c, :, :, :, pl.ds(0, width)].reshape(256, width).T

    st_a[0] = mine
    copies = [
        push(st_a.at[0], st_a.at[1 + n], z=step("z", k), c=step("c", e)) for n, (k, e) in enumerate(group)
    ]
    transpose_half(0)
    for copy in copies:
        copy.wait_recv()
    mine = merge([st_a[k] for k in range(8)])
    st_b[0] = mine
    copies = [
        push(st_b.at[0], st_b.at[1 + n], x=step("x", i), y=step("y", k)) for n, (i, k) in enumerate(plane)
    ]
    transpose_half(1)
    for copy in copies:
        copy.wait_recv()
    mine = merge([st_b[k] for k in range(16)])

    log_s = mine[0:1] + jnp.log(mine[1:2])
    log_t = mine[2:3] + jnp.log(mine[3:4])
    loss = mine[4:5] / mine[3:4] - log_t + log_s + CE_WEIGHT * (log_s - mine[5:6])
    columns = jnp.concatenate([log_s, log_t, loss, jnp.zeros((125, 256), F32)], axis=0).T
    grad = GRAD_SCALE * (
        (1.0 + CE_WEIGHT) * jnp.exp(logits[...] - columns[:, 0:1])
        - jnp.exp(teacher[...] - columns[:, 1:2])
        - CE_WEIGHT * hit.astype(F32)
    )
    grad_v[...] = grad.astype(BF16)

    own, to, came = (own_a, own_b, own_c), (to_a, to_b, to_c), (from_a, from_b, from_c)
    summed = (sum_a, sum_b, sum_c)
    fl, fr, rl, rr = (fl_a, fl_b, fl_c), (fr_a, fr_b, fr_c), (rl_a, rl_b, rl_c), (rr_a, rr_b, rr_c)
    widths = (SUM_BLOCK, SUM_WIDE // 2, SUM_WIDE // 2)
    first_of = (0, SUM_A, SUM_A + SUM_WIDE)
    crossing, ring_waits = {}, {}

    def partial_of(c, i, n):
        if i == 0:
            first = pl.multiple_of(step("z", Z_ORDER[n]) * SUM_BLOCK, 128)
        else:
            first = first_of[i] + n * widths[i]
        return lax.dot_general(
            grad_v[...], w_all[c, pl.ds(first, widths[i]), :], (((1,), (1,)), ((), ())),
            preferred_element_type=F32,
        ).reshape(4, 4, 16, widths[i])

    def pieces(i, n):
        return (2 * n, 2 * n + 1) if i == 0 else (n,)

    def send_unit(i, n):
        for p in pieces(i, n):
            to[i][p] = partial_of(other_core, i, p).astype(BF16)
        index = pl.ds(2 * n, 2) if i == 0 else n
        crossing[i, n] = push(to[i].at[index], came[i].at[index], c=other_core)

    def own_unit(i, n):
        for p in pieces(i, n):
            own[i][p] = partial_of(me["c"], i, p)

    def add_unit(i, n):
        crossing[i, n].wait_recv()
        for p in pieces(i, n):
            total = own[i][p] + came[i][p].astype(F32)
            own[i][p] = total
            summed[i][p] = total.astype(BF16)

    def block_of(i, k, n, half):
        if i == 0:
            return (Z_ORDER.index(k), half)
        if i == 1:
            return (n, step("x", k), half)
        return (n, half, step("y", k))

    def ring_push(i, k, n, half, buffer, toward):
        axis = ring_axis[i]
        place = () if i == 0 else (n,)
        if buffer is rl or buffer is rr:
            place = (*place, half)
        target = buffer[i].at[place] if place else buffer[i]
        return push(summed[i].at[block_of(i, k, n, half)], target, **{axis: step(axis, toward)})

    def ring_opposite(i, n):
        ring_waits[i, n] = [ring_push(i, 2, n, half0, fl, 1), ring_push(i, 2, n, half1, fr, 3)]

    def ring_up(i, n):
        ring_waits[i, n].append(ring_push(i, 1, n, half1, rl, 1))

    def ring_down(i, n):
        ring_waits[i, n].append(ring_push(i, 3, n, half0, rr, 3))

    def ring_forward(i, n):
        waits = ring_waits[i, n]
        for m, (k, half, ref, buffer) in enumerate(((1, half0, fl, rl), (3, half1, fr, rr))):
            waits[m].wait_recv()
            index = block_of(i, k, n, half)
            carried = ref[i][...] if i == 0 else ref[i][n]
            summed[i][index] = (own[i][index] + carried.astype(F32)).astype(BF16)
            waits.append(ring_push(i, k, n, half, buffer, k))

    def start_unit(i, n):
        ring_opposite(i, n)
        ring_up(i, n)
        ring_down(i, n)

    def start_last(i):
        axis = ring_axis[i]
        ring_waits[i, 1] = [None, None] + [
            push(summed[i].at[block_of(i, k, 1, full)], target, **{axis: step(axis, k)})
            for k, target in ((2, (None, ro_b, ro_c)[i]), (1, rl[i].at[1]), (3, rr[i].at[1]))
        ]

    def head_chunks(first, last):
        for n in range(first, last):
            chunk = pl.ds(n * CHUNK, CHUNK)
            head_out[chunk, :] = jnp.dot(ht[chunk, :], grad_v[...], preferred_element_type=F32).astype(BF16)

    send_unit(0, 0)
    send_unit(1, 0)
    send_unit(2, 0)
    own_unit(0, 0)
    send_unit(1, 1)
    own_unit(1, 0)
    send_unit(2, 1)
    add_unit(0, 0)
    ring_opposite(0, 0)
    ring_up(0, 0)
    send_unit(0, 1)
    add_unit(1, 0)
    start_unit(1, 0)
    own_unit(2, 0)
    add_unit(2, 0)
    start_unit(2, 0)
    own_unit(1, 1)
    add_unit(1, 1)
    start_last(1)
    own_unit(2, 1)
    add_unit(2, 1)
    start_last(2)
    own_unit(0, 1)
    add_unit(0, 1)
    ring_down(0, 0)
    ring_forward(0, 0)
    ring_forward(1, 0)
    ring_forward(2, 0)
    head_chunks(0, 3)

    def ring_done(i):
        for n in range(1 if i == 0 else 2):
            for copy in ring_waits[i, n][2:]:
                copy.wait_recv()

    ring_done(0)
    acc_a[...] = own_a[3] + rl_a[...].astype(F32) + rr_a[...].astype(F32)
    out_a[...] = acc_a[...].astype(BF16)
    wave_a = [
        push(out_a.at[step("x", i), step("y", k)], in_a.at[n], x=step("x", i), y=step("y", k))
        for n, (i, k) in enumerate(plane)
    ]
    ring_done(1)
    for n in range(2):
        cols = pl.ds(n * widths[1], widths[1])
        total = own_b[n, me["x"]] + rl_b[n].astype(F32) + rr_b[n].astype(F32)
        acc_b[:, :, cols] = total + ro_b[...].astype(F32) if n else total
    for z in range(4):
        piece = acc_b[:, pl.ds(z * 4, 4), :]
        keep_b[z] = piece
        out_b[z] = piece.astype(BF16)
    wave_b = [push(out_b.at[step("z", k)], in_b.at[k - 1], z=step("z", k)) for k in (2, 1, 3)]
    ring_done(2)
    for n in range(2):
        cols = pl.ds(n * widths[2], widths[2])
        total = own_c[n, :, me["y"]] + rl_c[n].astype(F32) + rr_c[n].astype(F32)
        acc_c[:, :, cols] = total + ro_c[...].astype(F32) if n else total
    out_c[...] = acc_c[...].astype(BF16)
    wave_c = [push(out_c.at[step("x", k)], in_c.at[k - 1], x=step("x", k)) for k in (2, 1, 3)]
    head_chunks(3, 6)
    loss_out[...] = jnp.broadcast_to(
        jnp.sum(jnp.where(reorder, columns[:, 2:3], 0.0), axis=0, keepdims=True), (8, 256)
    )

    for copy in wave_b:
        copy.wait_recv()
    total = keep_b[me["z"]]
    for n in range(3):
        total = total + in_b[n].astype(F32)
    for c in range(2):
        rest_b[:, c] = total[:, c * 2 : c * 2 + 2]

    def last_step(rest, last, axis):
        copies = [
            push(rest.at[step(axis, k), step("c", e)], last.at[e * 4 + k], **{axis: step(axis, k)}, c=step("c", e))
            for k, e in group
        ]
        last[0] = rest[me[axis], me["c"]]
        return copies

    wave_b = last_step(rest_b, last_b, "y")
    for copy in wave_c:
        copy.wait_recv()
    total = acc_c[me["x"]]
    for n in range(3):
        total = total + in_c[n].astype(F32)
    for z in range(4):
        for c in range(2):
            rest_c[z, c] = total[z * 4 + c * 2 : z * 4 + c * 2 + 2]
    wave_c = last_step(rest_c, last_c, "z")
    for copy in wave_a:
        copy.wait_recv()
    total = acc_a[me["x"], me["y"]]
    for n in range(15):
        total = total + in_a[n].astype(F32)
    for z in range(4):
        for c in range(2):
            rest_a[z, c] = total[z * 4 + c * 2 : z * 4 + c * 2 + 2]
    wave_a = []
    for k, e in group:
        z, c = step("z", k), step("c", e)
        wave_a.append(push(rest_a.at[z, c], last_a.at[me["z"], me["c"]], z=z, c=c))
    last_a[me["z"], me["c"]] = rest_a[me["z"], me["c"]]
    head_chunks(6, 8)

    for wave, last, first in ((wave_b, last_b, SUM_A), (wave_c, last_c, SUM_A + SUM_WIDE)):
        for copy in wave:
            copy.wait_recv()
        for e in range(2):
            total = last[e * 4] + last[e * 4 + 1] + last[e * 4 + 2] + last[e * 4 + 3]
            hg_out[step("c", e), :, pl.ds(first, SUM_WIDE)] = total
    for copy in wave_a:
        copy.wait_recv()
    for z in range(4):
        for c in range(2):
            hg_out[c, :, pl.ds(z * SUM_BLOCK, SUM_BLOCK)] = last_a[z, c]
    for copy in unsent:
        copy.wait_send()


def store_kernel(head_ref, hg_ref, loss_ref, head_out, hg_out, loss_out, sems):
    copies = []
    for n in range(8):
        chunk = pl.ds(n * CHUNK, CHUNK)
        copies.append(pltpu.make_async_copy(head_ref.at[chunk], head_out.at[chunk], sems.at[n]))
        copies[n].start()
    for c in range(2):
        hg_out[:, pl.ds(c * HALF, HALF)] = hg_ref[c]
    loss_out[...] = loss_ref[0]
    for copy in copies:
        copy.wait()


def per_device(hidden_states, head_weight, teacher_codes, teacher_scales, targets):
    codes = teacher_codes.reshape(2, 128, 512).transpose(1, 0, 2).reshape(2, 2, 4, 4, 2, 2, 512)
    weight = head_weight.reshape(2, HALF, 512)

    vmem = pltpu.VMEM
    unit_a, unit_b = (4, 4, 4, 16, SUM_BLOCK), (2, 4, 4, 16, SUM_WIDE // 2)
    forwarded_a, forwarded_b = (2, 4, 16, SUM_BLOCK), (2, 2, 16, SUM_WIDE // 2)
    arrived_a, arrived_b = (4, 4, 16, SUM_BLOCK), (2, 4, 16, SUM_WIDE // 2)
    units = (unit_a, unit_b, unit_b)
    forwarded, arrived = (forwarded_a, forwarded_b, forwarded_b), (arrived_a, arrived_b, arrived_b)
    scratch = [
        vmem((2, HALF, 512), BF16),
        vmem((256, 512), BF16),
        vmem((8192, 256), BF16),
        vmem((2, 2, HALF + 256), BF16),
        vmem((4, 2, 2, BLOCK_A), BF16),
        vmem((4, 4, 2, 2, WIDE), BF16),
        vmem((4, 4, 2, 2, WIDE), BF16),
        vmem((2, 4, 4, 4, 16, BLOCK_A), BF16),
        vmem((2, 4, 4, 16, WIDE), BF16),
        vmem((2, 4, 4, 16, WIDE), BF16),
        vmem((4, 2, 2, 4, 2, 2, 512), BF16),
        vmem((4, 4, 2, 4, 2, 512), BF16),
        vmem((4, 4, 4, 2, 2, 512), BF16),
        vmem((2, 4, 4, 4, 2, 512), BF16),
        vmem((256, 512), F32),
        vmem((256, 512), F32),
        vmem((8, 8, 256), F32),
        vmem((16, 8, 256), F32),
    ]
    scratch += [vmem(shape, F32) for shape in units]
    scratch += [vmem(shape, BF16) for shape in units * 3]
    scratch += [vmem(shape, BF16) for shape in forwarded * 2 + arrived * 2 + (arrived_b[1:],) * 2]
    scratch += [
        vmem((4, 4, 16, SUM_BLOCK), F32),
        vmem((4, 16, SUM_WIDE), F32),
        vmem((4, 16, SUM_WIDE), F32),
        vmem((4, 4, 16, SUM_BLOCK), BF16),
        vmem((4, 4, 4, SUM_WIDE), BF16),
        vmem((4, 16, SUM_WIDE), BF16),
        vmem((15, 16, SUM_BLOCK), BF16),
        vmem((3, 4, 4, SUM_WIDE), BF16),
        vmem((3, 16, SUM_WIDE), BF16),
        vmem((4, 4, 4, SUM_WIDE), F32),
        vmem((4, 2, 2, SUM_BLOCK), F32),
        vmem((4, 2, 2, SUM_WIDE), F32),
        vmem((4, 2, 2, SUM_WIDE), F32),
        vmem((4, 2, 2, SUM_BLOCK), F32),
        vmem((8, 2, SUM_WIDE), F32),
        vmem((8, 2, SUM_WIDE), F32),
        pltpu.SemaphoreType.DMA((248,)),
        pltpu.SemaphoreType.DMA((248,)),
        pltpu.SemaphoreType.DMA((8,)),
    ]
    hidden_grad, loss, head_grad = pl.pallas_call(
        kernel,
        out_shape=(
            pltpu.VMEM((2, 2, HALF), F32),
            pltpu.VMEM((8, 256), F32),
            pltpu.VMEM((8192, 512), BF16),
        ),
        in_specs=[pl.BlockSpec(memory_space=pltpu.HBM)] * 4 + [pl.BlockSpec(memory_space=pltpu.VMEM)],
        out_specs=[pl.BlockSpec(memory_space=pltpu.VMEM)] * 3,
        scratch_shapes=scratch,
        compiler_params=pltpu.CompilerParams(
            collective_id=0, has_side_effects=True, vmem_limit_bytes=57500000
        ),
    )(hidden_states, weight, codes, teacher_scales, targets.reshape(1, 256))

    head_grad, hidden_grad, token_loss = pl.pallas_call(
        store_kernel,
        out_shape=(
            jax.ShapeDtypeStruct((8192, 512), BF16),
            jax.ShapeDtypeStruct((2, 8192), F32),
            jax.ShapeDtypeStruct((256,), F32),
        ),
        in_specs=[pl.BlockSpec(memory_space=pltpu.VMEM)] * 3,
        out_specs=[pl.BlockSpec(memory_space=pltpu.HBM)] + [pl.BlockSpec(memory_space=pltpu.VMEM)] * 2,
        scratch_shapes=[pltpu.SemaphoreType.DMA((8,))],
        compiler_params=pltpu.CompilerParams(vmem_limit_bytes=40 * 1024 * 1024),
    )(head_grad, hidden_grad, loss)
    return hidden_grad, head_grad, token_loss


def solution(mesh):
    return jax.shard_map(
        per_device,
        mesh=mesh,
        in_specs=(
            P(AXES, None),
            P(None, AXES),
            P(AXES, None),
            P(AXES, None),
            P(),
        ),
        out_specs=(P(AXES, None), P(None, AXES), P()),
        check_vma=False,
    )
```

```python
import functools

import jax
import jax.numpy as jnp
from jax import lax
from jax.experimental import pallas as pl
from jax.experimental.pallas import tpu as pltpu
from jax.sharding import PartitionSpec as P

GRAD_SCALE = 32.0
CE_WEIGHT = 0.5
F32, BF16 = jnp.float32, jnp.bfloat16
MESH = pl.DeviceIdType.MESH
AXES = ("dp", "vocab")

CHUNK = 1024
HALF = 4096
BLOCK_A, PART_A, WIDE, HIDDEN_C = 128, 512, 1920, 1664
SUM_BLOCK, SUM_A, SUM_WIDE = 384, 1536, 1280
Z_ORDER = (2, 1, 3, 0)


def kernel(
    h_in, w_in, codes_in, scales_in, tgt_in,
    hg_out, loss_out, head_out,
    w_all, grad_v, ht, src, recv_a, rows_b, rows_c, h_a, h_b, h_c,
    t1, t2, t3, t4, logits, teacher, st_a, st_b,
    own_a, own_b, own_c, to_a, to_b, to_c, from_a, from_b, from_c, sum_a, sum_b, sum_c,
    fl_a, fl_b, fl_c, fr_a, fr_b, fr_c, rl_a, rl_b, rl_c, rr_a, rr_b, rr_c, ro_b, ro_c,
    acc_a, acc_b, acc_c, out_a, out_b, out_c, in_a, in_b, in_c, keep_b,
    rest_a, rest_b, rest_c, last_a, last_b, last_c,
    send_sems, recv_sems, local_sems,
):
    dp, vo = lax.axis_index("dp"), lax.axis_index("vocab")
    me = {"x": vo // 8, "z": (vo // 2) % 4, "y": (dp // 2) * 2 + vo % 2, "c": dp % 2}

    def device(**other):
        at = {**me, **other}
        return ((at["y"] // 2) * 2 + at["c"], (at["x"] * 4 + at["z"]) * 2 + at["y"] % 2)

    def step(axis, k):
        return lax.rem(me[axis] + k, 2 if axis == "c" else 4)

    count = {"remote": 0, "local": 0}
    unsent = []

    def push(src, dst, **other):
        n = count["remote"]
        count["remote"] += 1
        copy = pltpu.make_async_remote_copy(
            src_ref=src, dst_ref=dst, send_sem=send_sems.at[n], recv_sem=recv_sems.at[n],
            device_id=device(**other), device_id_type=MESH,
        )
        copy.start()
        unsent.append(copy)
        return copy

    def drain(keep=0):
        for copy in unsent[: len(unsent) - keep]:
            copy.wait_send()
        del unsent[: len(unsent) - keep]

    def local(src, dst):
        n = count["local"]
        count["local"] += 1
        copy = pltpu.make_async_copy(src, dst, local_sems.at[n])
        copy.start()
        return copy

    barrier = pltpu.get_barrier_semaphore()
    partners = [{axis: step(axis, k)} for axis in "xyz" for k in (2, 1, 3)]
    partners += [{axis: step(axis, k), "c": step("c", 1)} for axis in "yz" for k in (2, 1, 3)] + [dict(c=step("c", 1))]
    group = [(k, e) for k in range(4) for e in range(2) if (k, e) != (0, 0)]
    for other in partners:
        pl.semaphore_signal(barrier, inc=1, device_id=device(**other), device_id_type=MESH)

    heads = [local(h_in.at[:, pl.ds(c * HALF, HALF)], src.at[c, :, pl.ds(0, HALF)]) for c in range(2)]
    heads += [local(scales_in.at[:, pl.ds(c * 256, 256)], src.at[c, :, pl.ds(HALF, 256)]) for c in range(2)]
    own_codes = local(codes_in.at[:, :, me["x"]], t1.at[me["x"]])
    w_copy = local(w_in, w_all)
    k_row = lax.broadcasted_iota(jnp.int32, (256, 256), 0)
    n_col = lax.broadcasted_iota(jnp.int32, (256, 256), 1)
    natural = (
        ((k_row >> 5) & 1) * 128 + ((k_row >> 1) & 1) * 64 + (k_row >> 6) * 16
        + ((k_row >> 2) & 3) * 4 + ((k_row >> 4) & 1) * 2 + (k_row & 1)
    )
    reorder = natural == n_col
    target = jnp.sum(jnp.where(reorder, tgt_in[...].astype(F32), 0.0), axis=1, keepdims=True)
    first = (dp * 32 + vo) * 512
    hit = (first + lax.broadcasted_iota(jnp.int32, (256, 512), 1)).astype(F32) == target
    for copy in heads:
        copy.wait()
    pl.semaphore_wait(barrier, len(partners))

    other_core = step("c", 1)

    def spread(src_ref, dst_ref, axis):
        return [push(src_ref, dst_ref, **{axis: step(axis, k)}) for k in (2, 1, 3)]

    wave_a, wave_b, wave_c = [], [], []
    cols_b, cols_c = pl.ds(PART_A, WIDE), pl.ds(PART_A + WIDE, WIDE)
    for k, e in group:
        y, z, c = step("y", k), step("z", k), step("c", e)
        wave_b.append(push(src.at[c, :, cols_b], rows_b.at[me["y"], me["z"], me["c"]], y=y, c=c))
        wave_c.append(push(src.at[c, :, cols_c], rows_c.at[me["x"], me["z"], me["c"]], z=z, c=c))
        cols_a = pl.ds(pl.multiple_of(z * BLOCK_A, BLOCK_A), BLOCK_A)
        wave_a.append(push(src.at[c, :, cols_a], recv_a.at[me["z"], me["c"]], z=z, c=c))
    codes_wave = [push(codes_in.at[:, :, step("x", k)], t1.at[me["x"]], x=step("x", k)) for k in (2, 1, 3)]
    rows_b[me["y"], me["z"], me["c"]] = src[me["c"], :, cols_b]
    rows_c[me["x"], me["z"], me["c"]] = src[me["c"], :, cols_c]
    recv_a[me["z"], me["c"]] = src[me["c"], :, pl.ds(pl.multiple_of(me["z"] * BLOCK_A, BLOCK_A), BLOCK_A)]

    def pack(pieces):
        return jnp.concatenate([p.astype(F32) for p in pieces], axis=0).astype(BF16)

    own_codes.wait()

    for copy in wave_b:
        copy.wait_recv()
    wave_b = spread(rows_b.at[:, me["z"]], rows_b.at[:, me["z"]], "z")
    for copy in wave_c:
        copy.wait_recv()
    h_c[me["c"], me["x"], me["y"]] = pack([rows_c[me["x"], z, c] for z in range(4) for c in range(2)])
    view = h_c.at[me["c"], me["x"], me["y"]]
    wave_c = spread(view, view, "x")
    for copy in wave_a:
        copy.wait_recv()
    h_a[me["c"], me["z"], me["x"], me["y"]] = pack([recv_a[z, c] for z in range(4) for c in range(2)])
    view = h_a.at[me["c"], me["z"], me["x"], me["y"]]
    plane = [(i, k) for i in range(4) for k in range(4) if (i, k) != (0, 0)]
    wave_a = [push(view, view, x=step("x", i), y=step("y", k)) for i, k in plane]
    for copy in codes_wave:
        copy.wait_recv()
    codes_wave = [
        push(t1.at[:, step("y", k) // 2, :, :, step("y", k) % 2], t2.at[me["y"]], y=step("y", k))
        for k in (2, 1, 3)
    ]
    t2[me["y"]] = t1[:, me["y"] // 2, :, :, me["y"] % 2]

    full, half0, half1 = slice(None), pl.ds(0, 2), pl.ds(2, 2)
    ring_axis = ("z", "x", "y")

    def block(i, coordinate, half):
        if i == 0:
            return h_a.at[me["c"], coordinate, half]
        if i == 1:
            return h_b.at[me["c"], coordinate, half]
        return h_c.at[me["c"], half, coordinate]

    def ring(i, coordinate, half, k):
        view, axis = block(i, coordinate, half), ring_axis[i]
        return push(view, view, **{axis: step(axis, k)})

    crossing, right, left = [], [None] * 3, [None] * 3

    def cross(i, coordinate, half=full):
        view = block(i, coordinate, half)
        crossing.append(push(view, view, c=other_core))

    def start_ring(i):
        here = me[ring_axis[i]]
        right[i], left[i] = [], []
        for n in range(2):
            right[i].append(ring(i, here, n, 1))
            left[i].append(ring(i, here, 3 - n, 3))
        right[i].append(ring(i, here, half1, 1))
        left[i].append(ring(i, here, half0, 3))

    for copy in wave_c:
        copy.wait_recv()
    start_ring(2)
    for copy in codes_wave:
        copy.wait_recv()
    codes_wave = [push(t2.at[:, :, :, step("z", k)], t3.at[me["z"]], z=step("z", k)) for k in (2, 1, 3)]
    t3[me["z"]] = t2[:, :, :, me["z"]]
    for copy in wave_b:
        copy.wait_recv()
    for y in range(4):
        h_b[me["c"], me["x"], y] = pack([rows_b[y, z, c] for z in range(4) for c in range(2)])
    start_ring(1)
    for copy in wave_a:
        copy.wait_recv()
    start_ring(0)
    for i in (2, 1, 0):
        cross(i, me[ring_axis[i]])
    forward = [[], [], []]
    for n in range(2):
        for i in (2, 1, 0):
            right[i][n].wait_recv()
            forward[i].append(ring(i, step(ring_axis[i], 3), n, 1))
            left[i][n].wait_recv()
            forward[i].append(ring(i, step(ring_axis[i], 1), 3 - n, 3))
    for i in (2, 1, 0):
        right[i][2].wait_recv()
        cross(i, step(ring_axis[i], 3))
        left[i][2].wait_recv()
        cross(i, step(ring_axis[i], 1))
    for copy in codes_wave:
        copy.wait_recv()
    codes_core = push(t3.at[:, :, :, other_core], t4.at[me["c"]], c=other_core)
    t4[me["c"]] = t3[:, :, :, me["c"]]
    for i in (2, 1, 0):
        for copy in forward[i]:
            copy.wait_recv()
        cross(i, step(ring_axis[i], 2))

    w_copy.wait()
    logits[...] = jnp.zeros_like(logits)

    def add_logits(c):
        for ref, first, width in ((h_b, PART_A, WIDE), (h_c, PART_A + WIDE, HIDDEN_C)):
            rows = ref[c, :, :, :, pl.ds(0, width)].reshape(256, width)
            logits[...] += jnp.dot(rows, w_all[c, pl.ds(first, width), :], preferred_element_type=F32)
        rows = jnp.concatenate([h_a[c, z].reshape(256, BLOCK_A) for z in range(4)], axis=1)
        logits[...] += jnp.dot(rows, w_all[c, pl.ds(0, PART_A), :], preferred_element_type=F32)

    add_logits(me["c"])
    codes_core.wait_recv()
    for x in range(4):
        for y in range(4):
            teacher[pl.ds((x * 4 + y) * 16, 16), :] = jnp.concatenate(
                [t4[c, z, y, x].astype(F32) for z in range(4) for c in range(2)], axis=0
            )
    for copy in crossing:
        copy.wait_recv()
    block_row = lax.broadcasted_iota(jnp.int32, (256, 512), 0)
    column = lax.broadcasted_iota(jnp.int32, (256, 512), 1)
    pick = (block_row == (dp % 2) * 128 + vo * 4 + column // 128).astype(F32).astype(BF16)
    scales = h_c[dp // 2, :, :, :, pl.ds(HIDDEN_C, 256)].reshape(256, 256)
    teacher[...] *= jnp.dot(scales, pick, preferred_element_type=F32)
    add_logits(other_core)

    lg, tc = logits[...], teacher[...]
    m_s = jnp.max(lg, axis=1, keepdims=True)
    m_t = jnp.max(tc, axis=1, keepdims=True)
    w_t = jnp.exp(tc - m_t)
    stats = (
        m_s, jnp.sum(jnp.exp(lg - m_s), axis=1, keepdims=True),
        m_t, jnp.sum(w_t, axis=1, keepdims=True),
        jnp.sum(w_t * (tc - lg), axis=1, keepdims=True),
        jnp.sum(jnp.where(hit, lg, 0.0), axis=1, keepdims=True),
    )
    lane = lax.broadcasted_iota(jnp.int32, (256, 128), 1)
    packed = jnp.zeros((256, 128), F32)
    for n, value in enumerate(stats):
        packed = jnp.where(lane == n, value, packed)
    mine = packed.T[:8]

    def merge(parts):
        m1 = functools.reduce(jnp.maximum, [p[0:1] for p in parts])
        m2 = functools.reduce(jnp.maximum, [p[2:3] for p in parts])
        e1 = [jnp.exp(p[0:1] - m1) for p in parts]
        e2 = [jnp.exp(p[2:3] - m2) for p in parts]
        s1 = sum(p[1:2] * e for p, e in zip(parts, e1))
        s2 = sum(p[3:4] * e for p, e in zip(parts, e2))
        cross_sum = sum(p[4:5] * e for p, e in zip(parts, e2))
        target = sum(p[5:6] for p in parts)
        pad = jnp.zeros((2, 256), F32)
        return jnp.concatenate([m1, s1, m2, s2, cross_sum, target, pad], axis=0)

    def transpose_half(c):
        for z in range(4):
            ht[pl.ds(c * HALF + z * BLOCK_A, BLOCK_A), :] = h_a[c, z].reshape(256, BLOCK_A).T
        for ref, first, width in ((h_b, PART_A, WIDE), (h_c, PART_A + WIDE, HIDDEN_C)):
            ht[pl.ds(c * HALF + first, width), :] = ref[c, :, :, :, pl.ds(0, width)].reshape(256, width).T

    st_a[0] = mine
    copies = [
        push(st_a.at[0], st_a.at[1 + n], z=step("z", k), c=step("c", e)) for n, (k, e) in enumerate(group)
    ]
    drain(len(copies))
    transpose_half(0)
    for copy in copies:
        copy.wait_recv()
    mine = merge([st_a[k] for k in range(8)])
    st_b[0] = mine
    copies = [
        push(st_b.at[0], st_b.at[1 + n], x=step("x", i), y=step("y", k)) for n, (i, k) in enumerate(plane)
    ]
    drain(len(copies))
    transpose_half(1)
    for copy in copies:
        copy.wait_recv()
    mine = merge([st_b[k] for k in range(16)])

    log_s = mine[0:1] + jnp.log(mine[1:2])
    log_t = mine[2:3] + jnp.log(mine[3:4])
    loss = mine[4:5] / mine[3:4] - log_t + log_s + CE_WEIGHT * (log_s - mine[5:6])
    columns = jnp.concatenate([log_s, log_t, loss, jnp.zeros((125, 256), F32)], axis=0).T
    grad = GRAD_SCALE * (
        (1.0 + CE_WEIGHT) * jnp.exp(logits[...] - columns[:, 0:1])
        - jnp.exp(teacher[...] - columns[:, 1:2])
        - CE_WEIGHT * hit.astype(F32)
    )
    grad_v[...] = grad.astype(BF16)

    own, to, came = (own_a, own_b, own_c), (to_a, to_b, to_c), (from_a, from_b, from_c)
    summed = (sum_a, sum_b, sum_c)
    fl, fr, rl, rr = (fl_a, fl_b, fl_c), (fr_a, fr_b, fr_c), (rl_a, rl_b, rl_c), (rr_a, rr_b, rr_c)
    widths = (SUM_BLOCK, SUM_WIDE // 2, SUM_WIDE // 2)
    first_of = (0, SUM_A, SUM_A + SUM_WIDE)
    crossing, ring_waits = {}, {}

    def partial_of(c, i, n):
        if i == 0:
            first = pl.multiple_of(step("z", Z_ORDER[n]) * SUM_BLOCK, 128)
        else:
            first = first_of[i] + n * widths[i]
        return lax.dot_general(
            grad_v[...], w_all[c, pl.ds(first, widths[i]), :], (((1,), (1,)), ((), ())),
            preferred_element_type=F32,
        ).reshape(4, 4, 16, widths[i])

    def pieces(i, n):
        return (2 * n, 2 * n + 1) if i == 0 else (n,)

    def send_unit(i, n):
        for p in pieces(i, n):
            to[i][p] = partial_of(other_core, i, p).astype(BF16)
        index = pl.ds(2 * n, 2) if i == 0 else n
        crossing[i, n] = push(to[i].at[index], came[i].at[index], c=other_core)

    def own_unit(i, n):
        for p in pieces(i, n):
            own[i][p] = partial_of(me["c"], i, p)

    def add_unit(i, n):
        crossing[i, n].wait_recv()
        for p in pieces(i, n):
            total = own[i][p] + came[i][p].astype(F32)
            own[i][p] = total
            summed[i][p] = total.astype(BF16)

    def block_of(i, k, n, half):
        if i == 0:
            return (Z_ORDER.index(k), half)
        if i == 1:
            return (n, step("x", k), half)
        return (n, half, step("y", k))

    def ring_push(i, k, n, half, buffer, toward):
        axis = ring_axis[i]
        place = () if i == 0 else (n,)
        if buffer is rl or buffer is rr:
            place = (*place, half)
        target = buffer[i].at[place] if place else buffer[i]
        return push(summed[i].at[block_of(i, k, n, half)], target, **{axis: step(axis, toward)})

    def ring_opposite(i, n):
        ring_waits[i, n] = [ring_push(i, 2, n, half0, fl, 1), ring_push(i, 2, n, half1, fr, 3)]

    def ring_up(i, n):
        ring_waits[i, n].append(ring_push(i, 1, n, half1, rl, 1))

    def ring_down(i, n):
        ring_waits[i, n].append(ring_push(i, 3, n, half0, rr, 3))

    def ring_forward(i, n):
        waits = ring_waits[i, n]
        for m, (k, half, ref, buffer) in enumerate(((1, half0, fl, rl), (3, half1, fr, rr))):
            waits[m].wait_recv()
            index = block_of(i, k, n, half)
            carried = ref[i][...] if i == 0 else ref[i][n]
            summed[i][index] = (own[i][index] + carried.astype(F32)).astype(BF16)
            waits.append(ring_push(i, k, n, half, buffer, k))

    def start_unit(i, n):
        ring_opposite(i, n)
        ring_up(i, n)
        ring_down(i, n)

    def start_last(i):
        axis = ring_axis[i]
        ring_waits[i, 1] = [None, None] + [
            push(summed[i].at[block_of(i, k, 1, full)], target, **{axis: step(axis, k)})
            for k, target in ((2, (None, ro_b, ro_c)[i]), (1, rl[i].at[1]), (3, rr[i].at[1]))
        ]

    def head_chunks(first, last):
        for n in range(first, last):
            chunk = pl.ds(n * CHUNK, CHUNK)
            head_out[chunk, :] = jnp.dot(ht[chunk, :], grad_v[...], preferred_element_type=F32).astype(BF16)

    send_unit(0, 0)
    send_unit(1, 0)
    send_unit(2, 0)
    own_unit(0, 0)
    send_unit(1, 1)
    own_unit(1, 0)
    send_unit(2, 1)
    add_unit(0, 0)
    ring_opposite(0, 0)
    ring_up(0, 0)
    send_unit(0, 1)
    add_unit(1, 0)
    start_unit(1, 0)
    own_unit(2, 0)
    add_unit(2, 0)
    start_unit(2, 0)
    own_unit(1, 1)
    add_unit(1, 1)
    start_last(1)
    own_unit(2, 1)
    add_unit(2, 1)
    start_last(2)
    own_unit(0, 1)
    add_unit(0, 1)
    ring_down(0, 0)
    ring_forward(0, 0)
    ring_forward(1, 0)
    ring_forward(2, 0)
    head_chunks(0, 3)

    def ring_done(i):
        for n in range(1 if i == 0 else 2):
            for copy in ring_waits[i, n][2:]:
                copy.wait_recv()

    ring_done(0)
    acc_a[...] = own_a[3] + rl_a[...].astype(F32) + rr_a[...].astype(F32)
    out_a[...] = acc_a[...].astype(BF16)
    wave_a = [
        push(out_a.at[step("x", i), step("y", k)], in_a.at[n], x=step("x", i), y=step("y", k))
        for n, (i, k) in enumerate(plane)
    ]
    ring_done(1)
    for n in range(2):
        cols = pl.ds(n * widths[1], widths[1])
        total = own_b[n, me["x"]] + rl_b[n].astype(F32) + rr_b[n].astype(F32)
        acc_b[:, :, cols] = total + ro_b[...].astype(F32) if n else total
    for z in range(4):
        piece = acc_b[:, pl.ds(z * 4, 4), :]
        keep_b[z] = piece
        out_b[z] = piece.astype(BF16)
    wave_b = [push(out_b.at[step("z", k)], in_b.at[k - 1], z=step("z", k)) for k in (2, 1, 3)]
    ring_done(2)
    for n in range(2):
        cols = pl.ds(n * widths[2], widths[2])
        total = own_c[n, :, me["y"]] + rl_c[n].astype(F32) + rr_c[n].astype(F32)
        acc_c[:, :, cols] = total + ro_c[...].astype(F32) if n else total
    out_c[...] = acc_c[...].astype(BF16)
    wave_c = [push(out_c.at[step("x", k)], in_c.at[k - 1], x=step("x", k)) for k in (2, 1, 3)]
    drain(len(wave_a) + len(wave_b) + len(wave_c))
    head_chunks(3, 6)
    loss_out[...] = jnp.broadcast_to(
        jnp.sum(jnp.where(reorder, columns[:, 2:3], 0.0), axis=0, keepdims=True), (8, 256)
    )

    for copy in wave_b:
        copy.wait_recv()
    total = keep_b[me["z"]]
    for n in range(3):
        total = total + in_b[n].astype(F32)
    for c in range(2):
        rest_b[:, c] = total[:, c * 2 : c * 2 + 2]

    def last_step(rest, last, axis):
        copies = [
            push(rest.at[step(axis, k), step("c", e)], last.at[e * 4 + k], **{axis: step(axis, k)}, c=step("c", e))
            for k, e in group
        ]
        last[0] = rest[me[axis], me["c"]]
        return copies

    wave_b = last_step(rest_b, last_b, "y")
    for copy in wave_c:
        copy.wait_recv()
    total = acc_c[me["x"]]
    for n in range(3):
        total = total + in_c[n].astype(F32)
    for z in range(4):
        for c in range(2):
            rest_c[z, c] = total[z * 4 + c * 2 : z * 4 + c * 2 + 2]
    wave_c = last_step(rest_c, last_c, "z")
    for copy in wave_a:
        copy.wait_recv()
    total = acc_a[me["x"], me["y"]]
    for n in range(15):
        total = total + in_a[n].astype(F32)
    for z in range(4):
        for c in range(2):
            rest_a[z, c] = total[z * 4 + c * 2 : z * 4 + c * 2 + 2]
    wave_a = []
    for k, e in group:
        z, c = step("z", k), step("c", e)
        wave_a.append(push(rest_a.at[z, c], last_a.at[me["z"], me["c"]], z=z, c=c))
    last_a[me["z"], me["c"]] = rest_a[me["z"], me["c"]]
    drain(len(wave_a) + len(wave_b) + len(wave_c))
    head_chunks(6, 8)

    for wave, last, first in ((wave_b, last_b, SUM_A), (wave_c, last_c, SUM_A + SUM_WIDE)):
        for copy in wave:
            copy.wait_recv()
        for e in range(2):
            total = last[e * 4] + last[e * 4 + 1] + last[e * 4 + 2] + last[e * 4 + 3]
            hg_out[step("c", e), :, pl.ds(first, SUM_WIDE)] = total
    for copy in wave_a:
        copy.wait_recv()
    for z in range(4):
        for c in range(2):
            hg_out[c, :, pl.ds(z * SUM_BLOCK, SUM_BLOCK)] = last_a[z, c]
    drain()


def store_kernel(head_ref, hg_ref, loss_ref, head_out, hg_out, loss_out, sems):
    copies = []
    for n in range(8):
        chunk = pl.ds(n * CHUNK, CHUNK)
        copies.append(pltpu.make_async_copy(head_ref.at[chunk], head_out.at[chunk], sems.at[n]))
        copies[n].start()
    for c in range(2):
        hg_out[:, pl.ds(c * HALF, HALF)] = hg_ref[c]
    loss_out[...] = loss_ref[0]
    for copy in copies:
        copy.wait()


def per_device(hidden_states, head_weight, teacher_codes, teacher_scales, targets):
    codes = teacher_codes.reshape(2, 128, 512).transpose(1, 0, 2).reshape(2, 2, 4, 4, 2, 2, 512)
    weight = head_weight.reshape(2, HALF, 512)

    vmem = pltpu.VMEM
    unit_a, unit_b = (4, 4, 4, 16, SUM_BLOCK), (2, 4, 4, 16, SUM_WIDE // 2)
    forwarded_a, forwarded_b = (2, 4, 16, SUM_BLOCK), (2, 2, 16, SUM_WIDE // 2)
    arrived_a, arrived_b = (4, 4, 16, SUM_BLOCK), (2, 4, 16, SUM_WIDE // 2)
    units = (unit_a, unit_b, unit_b)
    forwarded, arrived = (forwarded_a, forwarded_b, forwarded_b), (arrived_a, arrived_b, arrived_b)
    scratch = [
        vmem((2, HALF, 512), BF16),
        vmem((256, 512), BF16),
        vmem((8192, 256), BF16),
        vmem((2, 2, HALF + 256), BF16),
        vmem((4, 2, 2, BLOCK_A), BF16),
        vmem((4, 4, 2, 2, WIDE), BF16),
        vmem((4, 4, 2, 2, WIDE), BF16),
        vmem((2, 4, 4, 4, 16, BLOCK_A), BF16),
        vmem((2, 4, 4, 16, WIDE), BF16),
        vmem((2, 4, 4, 16, WIDE), BF16),
        vmem((4, 2, 2, 4, 2, 2, 512), BF16),
        vmem((4, 4, 2, 4, 2, 512), BF16),
        vmem((4, 4, 4, 2, 2, 512), BF16),
        vmem((2, 4, 4, 4, 2, 512), BF16),
        vmem((256, 512), F32),
        vmem((256, 512), F32),
        vmem((8, 8, 256), F32),
        vmem((16, 8, 256), F32),
    ]
    scratch += [vmem(shape, F32) for shape in units]
    scratch += [vmem(shape, BF16) for shape in units * 3]
    scratch += [vmem(shape, BF16) for shape in forwarded * 2 + arrived * 2 + (arrived_b[1:],) * 2]
    scratch += [
        vmem((4, 4, 16, SUM_BLOCK), F32),
        vmem((4, 16, SUM_WIDE), F32),
        vmem((4, 16, SUM_WIDE), F32),
        vmem((4, 4, 16, SUM_BLOCK), BF16),
        vmem((4, 4, 4, SUM_WIDE), BF16),
        vmem((4, 16, SUM_WIDE), BF16),
        vmem((15, 16, SUM_BLOCK), BF16),
        vmem((3, 4, 4, SUM_WIDE), BF16),
        vmem((3, 16, SUM_WIDE), BF16),
        vmem((4, 4, 4, SUM_WIDE), F32),
        vmem((4, 2, 2, SUM_BLOCK), F32),
        vmem((4, 2, 2, SUM_WIDE), F32),
        vmem((4, 2, 2, SUM_WIDE), F32),
        vmem((4, 2, 2, SUM_BLOCK), F32),
        vmem((8, 2, SUM_WIDE), F32),
        vmem((8, 2, SUM_WIDE), F32),
        pltpu.SemaphoreType.DMA((248,)),
        pltpu.SemaphoreType.DMA((248,)),
        pltpu.SemaphoreType.DMA((8,)),
    ]
    hidden_grad, loss, head_grad = pl.pallas_call(
        kernel,
        out_shape=(
            pltpu.VMEM((2, 2, HALF), F32),
            pltpu.VMEM((8, 256), F32),
            pltpu.VMEM((8192, 512), BF16),
        ),
        in_specs=[pl.BlockSpec(memory_space=pltpu.HBM)] * 4 + [pl.BlockSpec(memory_space=pltpu.VMEM)],
        out_specs=[pl.BlockSpec(memory_space=pltpu.VMEM)] * 3,
        scratch_shapes=scratch,
        compiler_params=pltpu.CompilerParams(
            collective_id=0, has_side_effects=True, vmem_limit_bytes=57500000
        ),
    )(hidden_states, weight, codes, teacher_scales, targets.reshape(1, 256))

    head_grad, hidden_grad, token_loss = pl.pallas_call(
        store_kernel,
        out_shape=(
            jax.ShapeDtypeStruct((8192, 512), BF16),
            jax.ShapeDtypeStruct((2, 8192), F32),
            jax.ShapeDtypeStruct((256,), F32),
        ),
        in_specs=[pl.BlockSpec(memory_space=pltpu.VMEM)] * 3,
        out_specs=[pl.BlockSpec(memory_space=pltpu.HBM)] + [pl.BlockSpec(memory_space=pltpu.VMEM)] * 2,
        scratch_shapes=[pltpu.SemaphoreType.DMA((8,))],
        compiler_params=pltpu.CompilerParams(vmem_limit_bytes=40 * 1024 * 1024),
    )(head_grad, hidden_grad, loss)
    return hidden_grad, head_grad, token_loss


def solution(mesh):
    return jax.shard_map(
        per_device,
        mesh=mesh,
        in_specs=(
            P(AXES, None),
            P(None, AXES),
            P(AXES, None),
            P(AXES, None),
            P(),
        ),
        out_specs=(P(AXES, None), P(None, AXES), P()),
        check_vma=False,
    )
```
